128 devices in a mesh: row: 8 (over x, core), col: 16 (over z, y).
Axes of the slice: x: 4, y: 4, z: 4, core: 2. Of those that a mesh axis runs over, the one named last changes fastest.
Arguments:
- covariance: float32 [8, 8, 256, 16, 4, 256], P('row', None, None, 'col'), as said below
Outputs:
- factored: float32 [8, 8, 256, 16, 4, 256], P('row', None, None, 'col')
Inputs may be any that keep to these rules, and one draw needn't show every extreme that they name: covariance is symmetric and positive definite, a kernel matrix with a positive diagonal term.
All inputs are finite; a program needn't handle non-finite values.
Results may differ from the reference program's by a relative error of at most 0.0003.
Values sent between devices are 32-bit elements; how exact they have to be, the bound alone decides.
A program may use at most 128 MiB of HBM per device.

```python
import jax
import jax.numpy as jnp
from jax import lax

ORDER = 16384
NB = 256
STEPS = 2
GRID_ROWS = 8
GRID_COLS = 16
BR = 8
BC = 4


def draw_covariance(key, part):
    key = jax.random.fold_in(key, 11)
    key_place = jax.random.fold_in(key, 1)
    key_scale = jax.random.fold_in(key, 2)
    key_nugget = jax.random.fold_in(key, 3)
    positions = jax.random.uniform(key_place, (3, ORDER), jnp.float32)
    scales = jnp.exp(jax.random.uniform(key_scale, (ORDER,), jnp.float32, jnp.log(0.5), jnp.log(2.0)))
    length_scale = 0.25
    nugget = jnp.exp(jax.random.uniform(key_nugget, (ORDER,), jnp.float32, jnp.log(0.3), jnp.log(0.6)))
    distance = jnp.abs(positions[0][:, None] - positions[0][None, :])
    distance = distance + jnp.abs(positions[1][:, None] - positions[1][None, :])
    distance = distance + jnp.abs(positions[2][:, None] - positions[2][None, :])
    kernel = scales[:, None] * scales[None, :] * jnp.exp(-distance / length_scale)
    positions_index = jnp.arange(ORDER)
    kernel = kernel.at[positions_index, positions_index].add(nugget)
    return kernel.reshape(BR, GRID_ROWS, NB, BC, GRID_COLS, NB).transpose(1, 0, 2, 4, 3, 5)


def setup_inputs(seed: int = 0) -> dict:
    key_of = jax.random.split(jax.random.key(seed), 2)
    covariance = draw_covariance(jax.random.fold_in(key_of[1], 71), 0)
    return {"covariance": covariance}


def reference(covariance):
    covariance_full = jnp.transpose(covariance, (1, 0, 2, 4, 3, 5)).reshape(ORDER, ORDER)
    identity = jnp.eye(NB, dtype=jnp.float32)
    recorded = []
    for section in range(STEPS):
        start_index = section * NB
        end_index = start_index + NB
        factor_block = jnp.linalg.cholesky(covariance_full[start_index:end_index, start_index:end_index])
        inverse_t = jax.scipy.linalg.solve_triangular(factor_block, identity, lower=True).T
        panel_below = jnp.dot(covariance_full[end_index:, start_index:end_index], inverse_t, precision=lax.Precision.HIGHEST)
        product = jnp.dot(panel_below, panel_below.T, precision=lax.Precision.HIGHEST)
        covariance_full = covariance_full.at[end_index:, end_index:].add(-product)
        recorded.append((start_index, factor_block, panel_below))
    trailing_start = STEPS * NB
    result = covariance_full.at[:trailing_start, :].set(0.0).at[:, :trailing_start].set(0.0)
    for start_index, factor_block, panel_below in recorded:
        end_index = start_index + NB
        result = result.at[start_index:end_index, start_index:end_index].set(factor_block)
        result = result.at[end_index:, start_index:end_index].set(panel_below)
    return result.reshape(BR, GRID_ROWS, NB, BC, GRID_COLS, NB).transpose(1, 0, 2, 4, 3, 5)
```

```python
import functools

import jax
import jax.numpy as jnp
from jax import lax
from jax.experimental import pallas as pl
from jax.experimental.pallas import tpu as pltpu
from jax.sharding import PartitionSpec as P

F32 = jnp.float32
BF16 = jnp.bfloat16
HIGHEST = lax.Precision.HIGHEST
MESH = pl.DeviceIdType.MESH

PARENT = (
    (None, 5, 3, 0, 0, 4, 10, 4, 4, 10, 14, 10, 15, 14, 2, 14),
    (None, 2, 3, 0, 5, 9, 7, 3, 12, 8, 11, 7, 0, 9, 10, 11),
    (None, 0, 6, 7, 0, 4, 7, 4, 4, 8, 9, 7, 8, 12, 15, 12),
    (None, 0, 14, 15, 7, 1, 5, 3, 11, 13, 11, 15, 0, 12, 13, 12),
    (1, None, 6, 7, 7, 1, 5, 6, 9, 5, 6, 8, 8, 9, 10, 11),
    (1, None, 1, 15, 5, 6, 2, 6, 11, 5, 14, 15, 15, 14, 2, 14),
    (12, None, 14, 2, 8, 9, 10, 11, 9, 13, 9, 8, 13, 1, 13, 3),
    (3, None, 1, 2, 8, 6, 2, 11, 12, 10, 6, 10, 13, 1, 15, 3),
)
DIRS = ((1, 0), (-1, 0), (0, 1), (0, -1))


def step(n, dy, dz):
    return (n % 4 + dy) % 4 + ((n // 4 + dz) % 4) * 4


def depth_of(tree, n):
    d = 0
    while PARENT[tree][n] is not None:
        n = PARENT[tree][n]
        d += 1
    return d


DEPTH = tuple(tuple(depth_of(t, n) for n in range(16)) for t in range(8))
CHILD = tuple(
    tuple(tuple(int(PARENT[t][step(n, *d)] == n) for n in range(16)) for d in DIRS) for t in range(8)
)


def pick(n, table):
    value = jnp.int32(table[0])
    for i in range(1, len(table)):
        if table[i] != table[0]:
            value = jnp.where(n == i, jnp.int32(table[i]), value)
    return value


def wrap(v, m):
    return lax.rem(v + m, m)


CH = 64
NCH = 512 // CH
DR = 64
ND = 128 // DR
QR = 32
NQ = 128 // QR


class Links:
    def __init__(self, a_ref, pan, rows, diag, sems):
        self.a, self.pan, self.rows, self.diag = a_ref, pan, rows, diag
        (self.loc, self.d_send, self.d_recv, self.q_send, self.q_recv, self.p_send, self.p_recv) = sems
        self.row = lax.axis_index("row")
        self.n = lax.axis_index("col")
        self.x = self.row // 2
        self.core = lax.rem(self.row, 2)
        self.y = lax.rem(self.n, 4)
        self.z = self.n // 4

    def at(self, dx=0, dcore=0, dy=0, dz=0):
        return (
            wrap(self.x + dx, 4) * 2 + wrap(self.core + dcore, 2),
            wrap(self.z + dz, 4) * 4 + wrap(self.y + dy, 4),
        )

    def barrier(self):
        sem = pltpu.get_barrier_semaphore()
        peers = [dict(dx=d) for d in (1, 2, 3)] + [dict(dy=d) for d in (1, 2, 3)] + [dict(dz=d) for d in (1, 2, 3)]
        peers += [dict(dcore=1), dict(dcore=1, dy=1), dict(dcore=1, dy=-1)]
        for p in peers:
            pl.semaphore_signal(sem, inc=1, device_id=self.at(**p), device_id_type=MESH)
        pl.semaphore_wait(sem, len(peers))

    def panel_loads(self, k):
        out = []
        for r in range(8):
            for h in range(2):
                out.append(
                    pltpu.make_async_copy(
                        self.a.at[r, :, 4 * h, :],
                        self.pan.at[k, pl.ds(r * 256, 256), pl.ds(h * 128, 128)],
                        self.loc.at[r, h],
                    )
                )
        return out

    def row_load(self, k):
        return pltpu.make_async_copy(self.a.at[0], self.rows.at[k], self.loc.at[8, 0])

    def start_loads(self):
        for k in range(2):
            @pl.when(self.n == k)
            def _():
                for c in self.panel_loads(k):
                    c.start()

            @pl.when(self.row == k)
            def _():
                self.row_load(k).start()

    def wait_loads(self):
        for k in range(2):
            @pl.when(self.n == k)
            def _():
                for c in self.panel_loads(k):
                    c.wait()

            @pl.when(self.row == k)
            def _():
                self.row_load(k).wait()

    def d_copy(self, d, h, c, j, dev, src=None):
        part = self.diag.at[d, pl.ds(h * 128 + c * DR, DR)]
        return pltpu.make_async_remote_copy(
            part if src is None else src, part, self.d_send.at[d, h, c, j], self.d_recv.at[d, h, c], dev, device_id_type=MESH
        )

    def d_seed_copies(self, d, h, c):
        owner_core, k = ((0, 0), (1, 0), (1, 1))[d]
        src = self.pan.at[k, pl.ds(h * 128 + c * DR, DR)]
        if (owner_core, k) == (h, 0):
            return None, pltpu.make_async_copy(src, self.diag.at[d, pl.ds(h * 128 + c * DR, DR)], self.d_recv.at[d, h, c])
        return self.d_copy(d, h, c, 7, (h, 0), src), None

    def d_seed(self, d, wait=False):
        owner_core, k = ((0, 0), (1, 0), (1, 1))[d]

        @pl.when((self.row == owner_core) & (self.n == k))
        def _():
            for h in range(2):
                for c in range(ND):
                    remote, local = self.d_seed_copies(d, h, c)
                    if wait:
                        if remote is not None:
                            remote.wait_send()
                    elif remote is not None:
                        remote.start()
                    else:
                        local.start()

    def d_targets(self):
        out = []
        for j in (1, 3, 2):
            out.append(((self.n == 0) & (self.x == 0), self.at(dx=j)))
        for j in (1, 3, 2):
            out.append((self.n == 0, self.at(dy=j)))
        for j in (1, 3, 2):
            out.append((self.z == 0, self.at(dz=j)))
        return out

    def d_unit(self, d, c):
        for h in range(2):
            @pl.when(self.core == h)
            def _():
                self.d_copy(d, h, c, 0, self.at(dcore=1)).wait_recv()
                for i, (cond, dev) in enumerate(self.d_targets()):
                    @pl.when(cond)
                    def _(i=i, dev=dev):
                        self.d_copy(d, h, c, 8 + i, dev).start()
                self.d_copy(d, h, c, 0, self.at(dcore=1)).start()

    def d_other(self, d, c):
        for h in range(2):
            @pl.when(self.core != h)
            def _():
                self.d_copy(d, h, c, 0, self.at(dcore=1)).wait_recv()

    def d_drain(self):
        for d in range(3):
            for h in range(2):
                @pl.when(self.core == h)
                def _():
                    for c in range(ND):
                        for i, (cond, dev) in enumerate(self.d_targets()):
                            @pl.when(cond)
                            def _(i=i, dev=dev, c=c):
                                self.d_copy(d, h, c, 8 + i, dev).wait_send()
                        self.d_copy(d, h, c, 0, self.at(dcore=1)).wait_send()
            self.d_seed(d, wait=True)

    def q_copy(self, k, u, j, dev):
        part = self.rows.at[k, pl.ds(pl.multiple_of(u * QR, QR), QR)]
        return pltpu.make_async_remote_copy(part, part, self.q_send.at[u, j], self.q_recv.at[k, u], dev, device_id_type=MESH)

    def q_on(self, half):
        return (self.x != 3) if half == 0 else (self.x != 1)

    def q_round(self, i):
        for k in range(2):
            @pl.when(self.core == k)
            def _():
                for half in range(2):
                    depth = self.x if half == 0 else lax.rem(4 - self.x, 4)
                    c = i - depth

                    @pl.when((c >= 0) & (c < NQ))
                    def _(half=half, depth=depth, c=c):
                        u = half * NQ + c

                        @pl.when(depth > 0)
                        def _():
                            self.q_copy(k, u, 0, self.at(dcore=1)).wait_recv()

                        @pl.when(self.q_on(half))
                        def _():
                            self.q_copy(k, u, 1, self.at(dx=1 if half == 0 else -1)).start()

                        self.q_copy(k, u, 0, self.at(dcore=1)).start()

    def q_other(self):
        for k in range(2):
            @pl.when(self.core != k)
            def _():
                for u in range(2 * NQ):
                    self.q_copy(k, u, 0, self.at(dcore=1)).wait_recv()

    def q_drain(self):
        for k in range(2):
            @pl.when(self.core == k)
            def _():
                for half in range(2):
                    for c in range(NQ):
                        u = half * NQ + c
                        @pl.when(self.q_on(half))
                        def _(u=u):
                            self.q_copy(k, u, 1, self.at(dx=1 if half == 0 else -1)).wait_send()
                        self.q_copy(k, u, 0, self.at(dcore=1)).wait_send()

    def p_copy(self, t, q, j):
        part = self.pan.at[t // 4, pl.ds(pl.multiple_of((t % 4) * 512 + q * CH, CH), CH)]
        dy, dz = DIRS[j]
        return pltpu.make_async_remote_copy(
            part, part, self.p_send.at[t, j, q], self.p_recv.at[t, q], self.at(dy=dy, dz=dz), device_id_type=MESH
        )

    def p_tables(self):
        depth = [pick(self.n, DEPTH[t]) for t in range(8)]
        child = [[pick(self.n, CHILD[t][j]) for j in range(4)] for t in range(8)]
        return depth, child

    def p_round(self, i, tables):
        depth, child = tables
        for t in range(8):
            q = i - depth[t]

            @pl.when((q >= 0) & (q < NCH))
            def _():
                @pl.when(depth[t] > 0)
                def _():
                    self.p_copy(t, q, 0).wait_recv()
                for j in range(4):
                    @pl.when(child[t][j] == 1)
                    def _():
                        self.p_copy(t, q, j).start()

    def p_drain(self, tables):
        depth, child = tables
        for t in range(8):
            for j in range(4):
                @pl.when(child[t][j] == 1)
                def _():
                    def one(q, _):
                        self.p_copy(t, q, j).wait_send()
                        return 0
                    lax.fori_loop(0, NCH, one, 0)


ROUNDS = NCH + 5
QROUNDS = NQ + 3
SEMS = (
    pltpu.SemaphoreType.DMA((9, 2)),
    pltpu.SemaphoreType.DMA((3, 2, ND, 17)),
    pltpu.SemaphoreType.DMA((3, 2, ND)),
    pltpu.SemaphoreType.DMA((2 * NQ, 2)),
    pltpu.SemaphoreType.DMA((2, 2 * NQ)),
    pltpu.SemaphoreType.DMA((8, 4, NCH)),
    pltpu.SemaphoreType.DMA((8, NCH)),
)


def comm_kernel(a_ref, pan_out, rows_out, diag_out, pan, rows, diag, out_sem, *sems):
    net = Links(a_ref, pan, rows, diag, sems)
    net.start_loads()
    net.barrier()
    tables = net.p_tables()
    net.wait_loads()
    for d in range(3):
        net.d_seed(d)
    units = [(d, c) for d in range(3) for c in range(ND)]
    for i in range(ROUNDS):
        if i < len(units):
            net.d_unit(*units[i])
        net.p_round(i, tables)
        if i < QROUNDS:
            net.q_round(i)
    for u in units:
        net.d_other(*u)
    net.q_other()
    copies = [
        pltpu.make_async_copy(s, d, out_sem.at[i])
        for i, (s, d) in enumerate(((pan, pan_out), (rows, rows_out), (diag, diag_out)))
    ]
    for c in copies:
        c.start()
    net.d_drain()
    net.q_drain()
    net.p_drain(tables)
    for c in copies:
        c.wait()


def communicate(a):
    shapes = ((2, 2048, 256), (2, 256, 8, 128), (3, 256, 256))
    return pl.pallas_call(
        comm_kernel,
        out_shape=[jax.ShapeDtypeStruct(s, F32) for s in shapes],
        in_specs=[pl.BlockSpec(memory_space=pl.ANY)],
        out_specs=[pl.BlockSpec(memory_space=pl.ANY)] * 3,
        scratch_shapes=[pltpu.VMEM(s, F32) for s in shapes] + [pltpu.SemaphoreType.DMA((3,))] + list(SEMS),
        compiler_params=pltpu.CompilerParams(
            collective_id=0, has_side_effects=True, vmem_limit_bytes=48 * 2**20
        ),
        name="panels",
    )(a)


def split(x):
    hi = x.astype(BF16)
    return hi, (x - hi.astype(F32)).astype(BF16)


def mm(a, b, ta=False, precision=None):
    return lax.dot_general(
        a, b, (((0 if ta else 1,), (0,)), ((), ())), preferred_element_type=F32, precision=precision
    )


def mm3(a, b, ta=False):
    (ah, al), (bh, bl) = a, b
    return mm(ah, bh, ta) + (mm(ah, bl, ta) + mm(al, bh, ta))


def factor128(xa, xi, ta, ti):
    sub = lax.broadcasted_iota(jnp.int32, (8, 128), 0)

    def row(v, p):
        return jnp.broadcast_to(v[p : p + 1, :], (8, 128))

    def lane(v, c):
        return jnp.broadcast_to(v[:, c : c + 1], (8, 128))

    def total(s):
        return ((s[0] + s[1]) + (s[2] + s[3])) + ((s[4] + s[5]) + (s[6] + s[7]))

    for j in range(16):
        here = pl.ds(8 * j, 8)
        ra, ri = xa[here, :], xi[here, :]
        col = [lane(ra, 8 * j + k) for k in range(8)]
        la = jnp.zeros((8, 128), F32)
        li, rd = la, la
        for p in range(8):
            d = row(col[p], p)
            inv, root = 1.0 / d, lax.rsqrt(d)
            m = jnp.where(sub == p, 0.0, col[p] * inv)
            pa, pi = row(ra, p), row(ri, p)
            la = jnp.where(sub == p, pa * root, la)
            li = jnp.where(sub == p, pi * root, li)
            rd = jnp.where(sub == p, inv, rd)
            for k in range(p + 1, 8):
                col[k] = col[k] - m * row(col[k], p)
            ra, ri = ra - m * pa, ri - m * pi
        ta[here, :], ti[here, :] = la, li
        if j < 15:
            va, vi = ra * rd, ri * rd
            va = [row(va, k) for k in range(8)]
            vi = [row(vi, k) for k in range(8)]
            for g in range(j + 1, 16):
                there = pl.ds(8 * g, 8)
                xg = xa[there, :]
                c = [lane(xg, 8 * j + k) for k in range(8)]
                xa[there, :] = xg - total([c[k] * va[k] for k in range(8)])
                xi[there, :] = xi[there, :] - total([c[k] * vi[k] for k in range(8)])


def factor512(s, w, xa, xi, ta, ti):
    w[...] = jnp.zeros((512, 512), F32)
    i0 = lax.broadcasted_iota(jnp.int32, (128, 128), 0)
    i1 = lax.broadcasted_iota(jnp.int32, (128, 128), 1)

    def body(b, _):
        here = pl.ds(pl.multiple_of(b * 128, 128), 128)
        xa[...] = s[here, here]
        xi[...] = jnp.where(i0 == i1, 1.0, 0.0).astype(F32)
        factor128(xa, xi, ta, ti)
        w[here, here] = ti[...]
        s[here, here] = jnp.where(i1 >= i0, ta[...], 0.0)
        for bb in range(4):
            @pl.when(b == bb)
            def _(bb=bb):
                n0, n1 = bb * 128, bb * 128 + 128
                r = pl.ds(n0, 128)
                inv = ti[...]
                if bb > 0:
                    w[r, 0:n0] = mm(inv, w[r, 0:n0], precision=HIGHEST)
                if bb < 3:
                    u = mm(inv, s[r, n1:512], precision=HIGHEST)
                    s[r, n1:512] = u
                    s[n1:512, n1:512] = s[n1:512, n1:512] - mm(u, u, True, HIGHEST)
                    w[n1:512, 0:n1] = w[n1:512, 0:n1] - mm(u, w[r, 0:n1], True, HIGHEST)
        return 0

    lax.fori_loop(0, 4, body, 0)


def transposed_upper(s):
    i0 = lax.broadcasted_iota(jnp.int32, (256, 256), 0)
    i1 = lax.broadcasted_iota(jnp.int32, (256, 256), 1)
    return jnp.where(i1 >= i0, s, 0.0).T


def symmetrise(x):
    return (x + x.T) * 0.5


def load_diag(diag, s):
    s[0:256, 0:256] = symmetrise(diag[0])
    s[256:512, 0:256] = diag[1]
    s[0:256, 256:512] = diag[1].T
    s[256:512, 256:512] = symmetrise(diag[2])


def solve_rows(w, rows, n, mh, ml, t):
    w00, w10, w11 = split(w[0:256, 0:256]), split(w[256:512, 0:256]), split(w[256:512, 256:512])
    for q in range(8):
        ql = pl.ds(q * 128, 128)
        r0, r1 = split(rows[0, :, q, :]), split(rows[1, :, q, :])
        t0 = split(mm3(w00, r0))
        t1 = split(mm3(w10, r0) + mm3(w11, r1))
        m0 = mm3(w00, t0, True) + mm3(w10, t1, True)
        m1 = mm3(w11, t1, True)
        if q % 4 == 0:
            h = pl.ds((q // 4) * 128, 128)
            for k in range(2):
                wt = w[pl.ds(k * 256 + (q // 4) * 128, 128), :].T
                m0 = jnp.where(n == k, -wt[0:256], m0)
                m1 = jnp.where(n == k, -wt[256:512], m1)
        for i, m in enumerate((m0, m1)):
            hi, lo = split(m)
            mh[i * 256 : i * 256 + 256, ql] = hi
            ml[i * 256 : i * 256 + 256, ql] = lo


def solve_kernel(rows, diag, mh, ml, lower, s, w, xa, xi, ta, ti):
    load_diag(diag, s)
    factor512(s, w, xa, xi, ta, ti)
    lower[0] = transposed_upper(s[0:256, 0:256])
    lower[1] = transposed_upper(s[256:512, 256:512])
    solve_rows(w, rows, lax.axis_index("col"), mh, ml, None)


def solve(rows, diag):
    return pl.pallas_call(
        solve_kernel,
        out_shape=[
            jax.ShapeDtypeStruct((512, 1024), BF16),
            jax.ShapeDtypeStruct((512, 1024), BF16),
            jax.ShapeDtypeStruct((2, 256, 256), F32),
        ],
        scratch_shapes=[pltpu.VMEM((512, 512), F32)] * 2 + [pltpu.VMEM((128, 128), F32)] * 4,
        compiler_params=pltpu.CompilerParams(vmem_limit_bytes=40 * 2**20),
        name="factor",
    )(rows, diag)


RT = 512


def update_kernel(pan, mh, ml, lower, a, out):
    i = pl.program_id(0)
    row, n = lax.axis_index("row"), lax.axis_index("col")
    high, low = mh[...], ml[...]
    keep0 = jnp.where(n < 2, 0.0, 1.0).astype(F32)
    a2, o2 = a.reshape(RT * 8, 128), out.reshape(RT * 8, 128)
    p0, p1 = split(pan[0]), split(pan[1])
    top, bottom = pl.ds(0, 256), pl.ds(256, 256)
    m0 = (high[0:256], low[0:256])
    m1 = (high[256:512], low[256:512])
    prod = mm3(p0, m0) + mm3(p1, m1)
    for q in range(8):
        held = a2[pl.ds(q, RT, stride=8), :]
        if q % 4 == 0:
            held = held * keep0
        o2[pl.ds(q, RT, stride=8), :] = held - prod[:, q * 128 : q * 128 + 128]

    @pl.when((i == 0) & (row < 2))
    def _():
        for q in range(8):
            part = o2[pl.ds(q, 256, stride=8), :]
            if q % 4 == 0:
                h = (q // 4) * 128
                own = jnp.where(n == 0, lower[0, :, h : h + 128], lower[1, :, h : h + 128])
                part = jnp.where(row == n, own, jnp.where((row == 1) & (n == 0), part, 0.0))
            else:
                part = jnp.zeros_like(part)
            o2[pl.ds(q, 256, stride=8), :] = part


def update(pan, mh, ml, lower, a):
    whole = lambda *s: pl.BlockSpec(s, lambda i: (0,) * len(s))
    return pl.pallas_call(
        update_kernel,
        grid=(2048 // RT,),
        in_specs=[
            pl.BlockSpec((2, RT, 256), lambda i: (0, i, 0)),
            whole(512, 1024),
            whole(512, 1024),
            whole(2, 256, 256),
            pl.BlockSpec((RT, 8, 128), lambda i: (i, 0, 0)),
        ],
        out_specs=pl.BlockSpec((RT, 8, 128), lambda i: (i, 0, 0)),
        out_shape=jax.ShapeDtypeStruct((2048, 8, 128), F32),
        compiler_params=pltpu.CompilerParams(vmem_limit_bytes=50 * 2**20),
        name="update",
    )(pan, mh, ml, lower, a)


def shards(covariance):
    a = covariance.reshape(8, 256, 4, 2, 128).transpose(0, 1, 3, 2, 4).reshape(8, 256, 8, 128)
    pan, rows, diag = communicate(a)
    mh, ml, lower = solve(rows, diag)
    out = update(pan, mh, ml, lower, a.reshape(2048, 8, 128))
    return out.reshape(8, 256, 2, 4, 128).transpose(0, 1, 3, 2, 4).reshape(covariance.shape)


def solution(mesh):
    spec = P("row", None, None, "col", None, None)
    return jax.shard_map(shards, mesh=mesh, in_specs=(spec,), out_specs=spec, check_vma=False)
```

```python
import functools

import jax
import jax.numpy as jnp
from jax import lax
from jax.experimental import pallas as pl
from jax.experimental.pallas import tpu as pltpu
from jax.sharding import PartitionSpec as P

F32 = jnp.float32
BF16 = jnp.bfloat16
HIGHEST = lax.Precision.HIGHEST
MESH = pl.DeviceIdType.MESH

PARENT = (
    (None, 5, 3, 0, 0, 4, 10, 4, 4, 10, 14, 10, 15, 14, 2, 14),
    (None, 2, 3, 0, 5, 9, 7, 3, 12, 8, 11, 7, 0, 9, 10, 11),
    (None, 0, 6, 7, 0, 4, 7, 4, 4, 8, 9, 7, 8, 12, 15, 12),
    (None, 0, 14, 15, 7, 1, 5, 3, 11, 13, 11, 15, 0, 12, 13, 12),
    (1, None, 6, 7, 7, 1, 5, 6, 9, 5, 6, 8, 8, 9, 10, 11),
    (1, None, 1, 15, 5, 6, 2, 6, 11, 5, 14, 15, 15, 14, 2, 14),
    (12, None, 14, 2, 8, 9, 10, 11, 9, 13, 9, 8, 13, 1, 13, 3),
    (3, None, 1, 2, 8, 6, 2, 11, 12, 10, 6, 10, 13, 1, 15, 3),
)
DIRS = ((1, 0), (-1, 0), (0, 1), (0, -1))


def step(n, dy, dz):
    return (n % 4 + dy) % 4 + ((n // 4 + dz) % 4) * 4


def depth_of(tree, n):
    d = 0
    while PARENT[tree][n] is not None:
        n = PARENT[tree][n]
        d += 1
    return d


DEPTH = tuple(tuple(depth_of(t, n) for n in range(16)) for t in range(8))
CHILD = tuple(
    tuple(tuple(int(PARENT[t][step(n, *d)] == n) for n in range(16)) for d in DIRS) for t in range(8)
)
OFFSET = tuple(tuple(2 * d for d in row) for row in DEPTH)


def pick(n, table):
    value = jnp.int32(table[0])
    for i in range(1, len(table)):
        if table[i] != table[0]:
            value = jnp.where(n == i, jnp.int32(table[i]), value)
    return value


def wrap(v, m):
    return lax.rem(v + m, m)


CH = 32
NCH = 512 // CH
PG = 4
DU = 64
NDU = 256 // DU
ROUNDS = NCH + max(max(o) for o in OFFSET)
QSTEP = 3
DSTEP = 3


class Net:
    def __init__(self, a, pan, rows, diag, m, low, sems):
        self.a, self.pan, self.rows, self.diag, self.m, self.low = a, pan, rows, diag, m, low
        (self.load, self.seed, self.p_send, self.p_recv, self.g_send, self.g_recv, self.q_send, self.q_recv,
         self.d_send, self.d_recv, self.m_send, self.m_recv) = sems
        self.row = lax.axis_index("row")
        self.n = lax.axis_index("col")
        self.x = self.row // 2
        self.core = lax.rem(self.row, 2)
        self.y = lax.rem(self.n, 4)
        self.z = self.n // 4
        self.other = self.at(dcore=1)
        self.offset = [pick(self.n, OFFSET[t]) for t in range(8)]
        self.child = [[pick(self.n, CHILD[t][j]) for j in range(4)] for t in range(8)]

    def at(self, dx=0, dcore=0, dy=0, dz=0):
        return (
            wrap(self.x + dx, 4) * 2 + wrap(self.core + dcore, 2),
            wrap(self.z + dz, 4) * 4 + wrap(self.y + dy, 4),
        )

    def remote(self, part, send, recv, dev, src=None):
        return pltpu.make_async_remote_copy(
            part if src is None else src, part, send, recv, dev, device_id_type=MESH
        )

    def barrier(self):
        sem = pltpu.get_barrier_semaphore()
        peers = [dict(dcore=1)]
        peers += [dict(dx=d) for d in (1, 2, 3)] + [dict(dy=d) for d in (1, 2, 3)] + [dict(dz=d) for d in (1, 2, 3)]
        for p in peers:
            pl.semaphore_signal(sem, inc=1, device_id=self.at(**p), device_id_type=MESH)
        pl.semaphore_wait(sem, len(peers))

    def panel_load(self, k, c, t, h):
        return pltpu.make_async_copy(
            self.a.at[pl.ds(t * NCH, NCH), :, 4 * h, :],
            self.pan.at[k, t, :, c, :, pl.ds(h * 128, 128)],
            self.load.at[t, h],
        )

    def row_load(self, k):
        return pltpu.make_async_copy(self.a.at[pl.ds(0, 256 // CH)], self.rows.at[:, k], self.load.at[4, 0])

    def each_own(self, f):
        for k in range(2):
            for c in range(2):
                pl.when((self.n == k) & (self.core == c))(functools.partial(f, k, c))

    def start_loads(self):
        def panel(k, c):
            for t in range(4):
                for h in range(2):
                    self.panel_load(k, c, t, h).start()

        self.each_own(panel)
        for k in range(2):
            @pl.when(self.row == k)
            def _(k=k):
                self.row_load(k).start()

    def seed_copy(self, k, t):
        part = self.pan.at[k, t, :, 0]
        return self.remote(part, self.seed.at[t], self.g_recv.at[4 * k + t, 0], self.other)

    def d_part(self, u):
        return self.diag.at[u]

    def d_own(self, u):
        per = DU // CH
        return self.pan.at[1 if u // NDU == 2 else 0, 0, pl.ds((u % NDU) * per, per), 0 if u // NDU == 0 else 1]

    def wait_load(self, k, c, t):
        for h in range(2):
            self.panel_load(k, c, t, h).wait()

    def own_first(self):
        def panel(k, c):
            self.wait_load(k, c, 0)
            for d in range(3):
                if (c, k) == ((0, 0), (1, 0), (1, 1))[d]:
                    @pl.when(self.x == 0)
                    def _(d=d):
                        for u in range(d * NDU, d * NDU + NDU):
                            if d < 2:
                                pltpu.make_async_copy(self.d_own(u), self.d_part(u), self.d_recv.at[u]).start()
                            else:
                                self.d_seed(u).start()

        self.each_own(panel)

    def own_rest(self):
        def panel(k, c):
            for t in range(4):
                if t > 0:
                    self.wait_load(k, c, t)
                if c == 0:
                    self.seed_copy(k, t).start()

        self.each_own(panel)
        for k in range(2):
            @pl.when(self.row == k)
            def _(k=k):
                self.row_load(k).wait()
                self.row_copy(k).start()

    def row_copy(self, k):
        part = self.rows.at[:, k]
        return self.remote(part, self.q_send.at[8, k], self.q_recv.at[8], self.other)

    def d_seed(self, u):
        return self.remote(self.d_part(u), self.d_send.at[u, 9], self.d_recv.at[u], (1, 0), self.d_own(u))

    def d_targets(self, order):
        zero = {"x": self.x == 0, "y": self.y == 0, "z": self.z == 0}
        out = []
        for i, axis in enumerate(order):
            cond = None
            for rest in order[i:]:
                cond = zero[rest] if cond is None else cond & zero[rest]
            for step_ in (1, 3, 2):
                out.append((cond, self.at(**{"d" + axis: step_})))
        return out

    def d_copy(self, u, j, dev):
        return self.remote(self.d_part(u), self.d_send.at[u, j], self.d_recv.at[u], dev)

    def d_push(self, u):
        return self.d_copy(u, 10, self.other)

    def d_each(self, u, f):
        for i, order in enumerate(("xyz", "yzx", "zxy")):
            @pl.when(lax.rem(u, 3) == i)
            def _(order=order):
                for j, (cond, dev) in enumerate(self.d_targets(order)):
                    pl.when(cond)(functools.partial(f, j, dev))

    def d_unit(self, u):
        self.d_copy(u, 0, self.other).wait_recv()
        self.d_each(u, lambda j, dev: self.d_copy(u, j, dev).start())

    def d_first(self):
        def unit(u, _):
            self.d_unit(u)
            return 0

        lax.fori_loop(0, NDU, unit, 0)

    def d_round(self, i):
        hops = sum(jnp.where(v == 0, 0, 1).astype(jnp.int32) for v in (self.x, self.y, self.z))
        c = i - DSTEP * hops

        @pl.when((c >= 0) & (c < 2 * NDU))
        def _():
            u = c + NDU
            self.d_unit(u)
            self.d_push(u).start()

    def d_land(self):
        for u in range(NDU, 3 * NDU):
            self.d_push(u).wait_recv()

    def d_drain(self, lo, hi, push):
        def unit(u, _):
            self.d_each(u, lambda j, dev: self.d_copy(u, j, dev).wait_send())
            if push:
                self.d_push(u).wait_send()
            return 0

        lax.fori_loop(lo, hi, unit, 0)

    def q_copy(self, u, j, dev):
        return self.remote(self.rows.at[u], self.q_send.at[u, j], self.q_recv.at[u], dev)

    def q_on(self, half):
        return (self.x != 3) if half == 0 else (self.x != 1)

    def q_dev(self, half):
        return self.at(dx=1 if half == 0 else -1)

    def q_start(self):
        @pl.when(self.x == 0)
        def _():
            self.row_copy(0).wait_recv()

    def q_round(self, i):
        for half in range(2):
            depth = self.x if half == 0 else lax.rem(4 - self.x, 4)
            c = i - depth

            @pl.when((c >= 0) & (c < 4))
            def _(half=half, depth=depth, c=c):
                u = half * 4 + c

                @pl.when(depth > 0)
                def _():
                    self.q_copy(u, 0, self.other).wait_recv()
                    self.q_copy(u, 0, self.other).start()

                @pl.when(self.q_on(half))
                def _():
                    self.q_copy(u, 1, self.q_dev(half)).start()

    def q_drain(self):
        for half in range(2):
            def unit(c, _, half=half):
                u = half * 4 + c

                @pl.when(self.x > 0)
                def _():
                    self.q_copy(u, 0, self.other).wait_send()

                @pl.when(self.q_on(half))
                def _():
                    self.q_copy(u, 1, self.q_dev(half)).wait_send()

                return 0

            lax.fori_loop(0, 4, unit, 0)

    def q_land(self):
        @pl.when(self.x == 0)
        def _():
            self.row_copy(1).wait_recv()

        @pl.when(self.x > 0)
        def _():
            for u in range(8):
                self.q_copy(u, 0, self.other).wait_recv()

    def p_copy(self, t, q, j):
        dy, dz = DIRS[j]
        return self.remote(
            self.pan.at[t // 4, t % 4, q], self.p_send.at[t, j, q], self.p_recv.at[t, q], self.at(dy=dy, dz=dz)
        )

    def p_group(self, t, g):
        part = self.pan.at[t // 4, lax.rem(t, 4), pl.ds(g * PG, PG), 0]
        return self.remote(part, self.g_send.at[t, g], self.g_recv.at[t, g], self.other)

    def is_root(self, t):
        return self.n == t // 4

    def p_start(self):
        for k in range(2):
            @pl.when(self.n == k)
            def _(k=k):
                for t in range(4):
                    self.seed_copy(k, t).wait_recv()

    def p_round(self, i):
        for t in range(8):
            q = i - self.offset[t]

            @pl.when((q >= 0) & (q < NCH))
            def _(t=t, q=q):
                root = self.is_root(t)

                @pl.when(jnp.logical_not(root))
                def _():
                    self.p_copy(t, q, 0).wait_recv()

                for j in range(4):
                    @pl.when(self.child[t][j] == 1)
                    def _(j=j):
                        self.p_copy(t, q, j).start()

                @pl.when(jnp.logical_not(root) & (lax.rem(q, PG) == PG - 1))
                def _():
                    self.p_group(t, q // PG).start()

    def p_drain(self):
        for t in range(8):
            for j in range(4):
                @pl.when(self.child[t][j] == 1)
                def _(t=t, j=j):
                    def one(q, _):
                        self.p_copy(t, q, j).wait_send()
                        return 0
                    lax.fori_loop(0, NCH, one, 0)

            @pl.when(jnp.logical_not(self.is_root(t)))
            def _(t=t):
                for g in range(NCH // PG):
                    self.p_group(t, g).wait_send()

    def p_land(self, t):
        for k in range(2):
            @pl.when(self.n != k)
            def _(k=k):
                for g in range(NCH // PG):
                    self.p_group(4 * k + t, g).wait_recv()

    def own_drain(self):
        def panel(k, c):
            for d in (2,):
                if (c, k) == (1, 1):
                    @pl.when(self.x == 0)
                    def _(d=d):
                        for u in range(d * NDU, d * NDU + NDU):
                            self.d_seed(u).wait_send()
            if c == 0:
                for t in range(4):
                    self.seed_copy(k, t).wait_send()

        self.each_own(panel)
        for k in range(2):
            @pl.when(self.row == k)
            def _(k=k):
                self.row_copy(k).wait_send()

    def m_copy(self, i):
        return self.remote(self.m.at[i], self.m_send.at[i], self.m_recv.at[i], self.other)

    def low_copy(self):
        return self.remote(self.low.at[1], self.m_send.at[2], self.m_recv.at[2], self.other)


SEMS = (
    pltpu.SemaphoreType.DMA((5, 2)),
    pltpu.SemaphoreType.DMA((4,)),
    pltpu.SemaphoreType.DMA((8, 4, NCH)),
    pltpu.SemaphoreType.DMA((8, NCH)),
    pltpu.SemaphoreType.DMA((8, NCH // PG)),
    pltpu.SemaphoreType.DMA((8, NCH // PG)),
    pltpu.SemaphoreType.DMA((9, 2)),
    pltpu.SemaphoreType.DMA((9,)),
    pltpu.SemaphoreType.DMA((3 * NDU, 11)),
    pltpu.SemaphoreType.DMA((3 * NDU,)),
    pltpu.SemaphoreType.DMA((3,)),
    pltpu.SemaphoreType.DMA((3,)),
)


def split(x):
    hi = x.astype(BF16)
    return hi, (x - hi.astype(F32)).astype(BF16)


def mm(a, b, ta=False, precision=None):
    return lax.dot_general(
        a, b, (((0 if ta else 1,), (0,)), ((), ())), preferred_element_type=F32, precision=precision
    )


def mm3(a, b, ta=False):
    (ah, al), (bh, bl) = a, b
    return mm(ah, bh, ta) + (mm(ah, bl, ta) + mm(al, bh, ta))


def factor128(xa, xi, ta, ti):
    sub = lax.broadcasted_iota(jnp.int32, (8, 128), 0)

    def row(v, p):
        return jnp.broadcast_to(v[p : p + 1, :], (8, 128))

    def lane(v, c):
        return jnp.broadcast_to(v[:, c : c + 1], (8, 128))

    def total(s):
        return ((s[0] + s[1]) + (s[2] + s[3])) + ((s[4] + s[5]) + (s[6] + s[7]))

    first = xa[0:8, :]
    col = [lane(first, k) for k in range(8)]
    for j in range(16):
        here = pl.ds(8 * j, 8)
        ra, ri = xa[here, :], xi[here, :]
        last = j == 15
        if not last:
            nxt = xa[pl.ds(8 * j + 8, 8), :]
            b = [lane(nxt, 8 * j + k) for k in range(8)]
            ahead = [lane(nxt, 8 * j + 8 + k) for k in range(8)]
            below = list(b)
        la = jnp.zeros((8, 128), F32)
        li, rd = la, la
        for p in range(8):
            d = row(col[p], p)
            inv, root = 1.0 / d, lax.rsqrt(d)
            m = jnp.where(sub == p, 0.0, col[p] * inv)
            pa, pi = row(ra, p), row(ri, p)
            if p < 7:
                head = [row(col[k], p) for k in range(p + 1, 8)]
                for k in range(p + 1, 8):
                    col[k] = col[k] - m * head[k - p - 1]
            if not last:
                mb = b[p] * inv
                for k in range(p + 1, 8):
                    b[k] = b[k] - mb * head[k - p - 1]
                for k in range(8):
                    ahead[k] = ahead[k] - mb * row(b[p], k)
            la = jnp.where(sub == p, pa * root, la)
            li = jnp.where(sub == p, pi * root, li)
            rd = jnp.where(sub == p, inv, rd)
            ra, ri = ra - m * pa, ri - m * pi
        ta[here, :], ti[here, :] = la, li
        if not last:
            va, vi = ra * rd, ri * rd
            va = [row(va, k) for k in range(8)]
            vi = [row(vi, k) for k in range(8)]
            for g in range(j + 1, 16):
                there = pl.ds(8 * g, 8)
                xg = xa[there, :]
                c = below if g == j + 1 else [lane(xg, 8 * j + k) for k in range(8)]
                xa[there, :] = xg - total([c[k] * va[k] for k in range(8)])
                xi[there, :] = xi[there, :] - total([c[k] * vi[k] for k in range(8)])
            col = ahead


def factor512(s, w, xa, xi, ta, ti, join):
    w[...] = jnp.zeros((512, 512), F32)
    i0 = lax.broadcasted_iota(jnp.int32, (128, 128), 0)
    i1 = lax.broadcasted_iota(jnp.int32, (128, 128), 1)

    def body(b, _):
        here = pl.ds(pl.multiple_of(b * 128, 128), 128)
        xa[...] = s[here, here]
        xi[...] = jnp.where(i0 == i1, 1.0, 0.0).astype(F32)
        factor128(xa, xi, ta, ti)
        w[here, here] = ti[...]
        s[here, here] = jnp.where(i1 >= i0, ta[...], 0.0)
        for bb in range(4):
            @pl.when(b == bb)
            def _(bb=bb):
                n0, n1 = bb * 128, bb * 128 + 128
                r, rest = pl.ds(n0, 128), pl.ds(n1, 128)
                inv = ti[...]
                if bb > 0:
                    w[r, 0:n0] = mm(inv, w[r, 0:n0], precision=HIGHEST)
                if bb % 2 == 0:
                    u = mm(inv, s[r, rest], precision=HIGHEST)
                    s[r, rest] = u
                    s[rest, rest] = s[rest, rest] - mm(u, u, True, HIGHEST)
                    w[rest, 0:n1] = w[rest, 0:n1] - mm(u, w[r, 0:n1], True, HIGHEST)
                if bb == 1:
                    below, corner = join()
                    first = w[0:256, 0:256]
                    u = mm(first, below.T, precision=HIGHEST)
                    s[256:512, 256:512] = symmetrise(corner) - mm(u, u, True, HIGHEST)
                    w[256:512, 0:256] = -mm(u, first, True, HIGHEST)
        return 0

    lax.fori_loop(0, 4, body, 0)


def transposed_upper(s):
    i0 = lax.broadcasted_iota(jnp.int32, (256, 256), 0)
    i1 = lax.broadcasted_iota(jnp.int32, (256, 256), 1)
    return jnp.where(i1 >= i0, s, 0.0).T


def symmetrise(x):
    return (x + x.T) * 0.5


def block(diag, d):
    return diag[d * NDU : d * NDU + NDU].reshape(256, 256)


def gather_rows(rows, rh, rl):
    flat = rows.reshape(8 * 2 * CH * 8, 128)
    for k in range(2):
        for u in range(8):
            r = pl.ds(k * 256 + u * CH, CH)
            for q in range(8):
                hi, lo = split(flat[pl.ds((u * 2 + k) * CH * 8 + q, CH, stride=8), :])
                rh[r, q * 128 : q * 128 + 128] = hi
                rl[r, q * 128 : q * 128 + 128] = lo


def solve_rows(w, n, rh, rl, m, done):
    w00, w10, w11 = split(w[0:256, 0:256]), split(w[256:512, 0:256]), split(w[256:512, 256:512])
    for half in range(2):
        cols = pl.ds(half * 512, 512)
        r0, r1 = (rh[0:256, cols], rl[0:256, cols]), (rh[256:512, cols], rl[256:512, cols])
        t0 = split(mm3(w00, r0))
        t1 = split(mm3(w10, r0) + mm3(w11, r1))
        m[half, 0:256] = mm3(w00, t0, True) + mm3(w10, t1, True)
        m[half, 256:512] = mm3(w11, t1, True)
        for k in range(2):
            @pl.when(n == k)
            def _(k=k):
                m[half, :, 0:128] = -w[pl.ds(k * 256 + half * 128, 128), :].T
        done(half)


def update_tile(out, pan, m, core, t, half, keep):
    o2 = out.reshape(2048 * 8, 128)
    left = [split(pan[k, t, :, core].reshape(512, 256)) for k in range(2)]
    right = [split(m[half, k * 256 : k * 256 + 256]) for k in range(2)]
    prod = mm3(left[0], right[0]) + mm3(left[1], right[1])
    for q in range(4):
        there = pl.ds(t * 512 * 8 + half * 4 + q, 512, stride=8)
        held = o2[there, :]
        if q == 0:
            held = held * keep
        o2[there, :] = held - prod[:, q * 128 : q * 128 + 128]


def own_rows(out, low, row, n):
    o2 = out.reshape(2048 * 8, 128)
    for q in range(8):
        there = pl.ds(q, 256, stride=8)
        if q % 4:
            o2[there, :] = jnp.zeros((256, 128), F32)
        else:
            h = (q // 4) * 128
            own = jnp.where(n == 0, low[0, :, h : h + 128], low[1, :, h : h + 128])
            o2[there, :] = jnp.where(row == n, own, jnp.where((row == 1) & (n == 0), o2[there, :], 0.0))


def kernel(a, out, pan, rows, diag, s, w, low, xa, xi, ta, ti, rh, rl, m, a_sem, *sems):
    net = Net(a, pan, rows, diag, m, low, sems)
    net.start_loads()
    held = pltpu.make_async_copy(a, out, a_sem)
    held.start()
    net.barrier()
    net.own_first()
    source = (net.row == 0) & (net.n == 0)
    pl.when(source)(net.d_first)
    net.own_rest()
    keep = jnp.where(net.n < 2, 0.0, 1.0).astype(F32)

    @pl.when(net.core == 0)
    def _():
        pl.when(jnp.logical_not(source))(net.d_first)
        s[0:256, 0:256] = symmetrise(block(diag, 0))

        def join():
            net.d_land()
            return block(diag, 1), block(diag, 2)

        factor512(s, w, xa, xi, ta, ti, join)
        net.q_land()
        gather_rows(rows, rh, rl)
        solve_rows(w, net.n, rh, rl, m, lambda i: net.m_copy(i).start())
        low[0] = transposed_upper(s[0:256, 0:256])
        low[1] = transposed_upper(s[256:512, 256:512])
        net.low_copy().start()

    @pl.when(net.core == 1)
    def _():
        low[0] = jnp.zeros((256, 256), F32)
        net.p_start()
        net.q_start()

        def one(i, _):
            net.d_round(i)
            net.p_round(i)

            @pl.when(lax.rem(i, QSTEP) == 0)
            def _():
                net.q_round(i // QSTEP)

            return 0

        lax.fori_loop(0, ROUNDS, one, 0)
        for i in range(2):
            net.m_copy(i).wait_recv()

    held.wait()

    def tile(t, _):
        pl.when(net.core == 0)(lambda: net.p_land(t))
        for half in range(2):
            update_tile(out, pan, m, net.core, t, half, keep)
        return 0

    lax.fori_loop(0, 4, tile, 0)

    @pl.when(net.core == 1)
    def _():
        net.low_copy().wait_recv()

    @pl.when(net.row < 2)
    def _():
        own_rows(out, low, net.row, net.n)

    @pl.when(net.core == 0)
    def _():
        net.d_drain(0, NDU, False)
        for i in range(2):
            net.m_copy(i).wait_send()
        net.low_copy().wait_send()

    @pl.when(net.core == 1)
    def _():
        net.d_drain(NDU, 3 * NDU, True)
        net.p_drain()
        net.q_drain()

    net.own_drain()


def two_steps(a):
    return pl.pallas_call(
        kernel,
        out_shape=pltpu.VMEM(a.shape, F32),
        in_specs=[pl.BlockSpec(memory_space=pl.ANY)],
        out_specs=pl.BlockSpec(memory_space=pltpu.VMEM),
        scratch_shapes=[
            pltpu.VMEM((2, 4, NCH, 2, CH, 256), F32),
            pltpu.VMEM((8, 2, CH, 8, 128), F32),
            pltpu.VMEM((3 * NDU, DU // CH, CH, 256), F32),
            pltpu.VMEM((512, 512), F32),
            pltpu.VMEM((512, 512), F32),
            pltpu.VMEM((2, 256, 256), F32),
        ]
        + [pltpu.VMEM((128, 128), F32)] * 4
        + [pltpu.VMEM((512, 1024), BF16)] * 2
        + [pltpu.VMEM((2, 512, 512), F32), pltpu.SemaphoreType.DMA]
        + list(SEMS),
        compiler_params=pltpu.CompilerParams(
            collective_id=0, has_side_effects=True, vmem_limit_bytes=46 * 2**20
        ),
        name="steps",
    )(a)


def shards(covariance):
    a = covariance.reshape(8, 256, 4, 2, 128).transpose(0, 1, 3, 2, 4).reshape(2048 // CH, CH, 8, 128)
    out = two_steps(a)
    return out.reshape(8, 256, 2, 4, 128).transpose(0, 1, 3, 2, 4).reshape(covariance.shape)


def solution(mesh):
    spec = P("row", None, None, "col", None, None)
    return jax.shard_map(shards, mesh=mesh, in_specs=(spec,), out_specs=spec, check_vma=False)
```

```python
import functools

import jax
import jax.numpy as jnp
from jax import lax
from jax.experimental import pallas as pl
from jax.experimental.pallas import tpu as pltpu
from jax.sharding import PartitionSpec as P

F32 = jnp.float32
BF16 = jnp.bfloat16
HIGHEST = lax.Precision.HIGHEST
MESH = pl.DeviceIdType.MESH

PARENT = (
    (None, 5, 3, 0, 0, 4, 10, 4, 4, 10, 14, 10, 15, 14, 2, 14),
    (None, 2, 3, 0, 5, 9, 7, 3, 12, 8, 11, 7, 0, 9, 10, 11),
    (None, 0, 6, 7, 0, 4, 7, 4, 4, 8, 9, 7, 8, 12, 15, 12),
    (None, 0, 14, 15, 7, 1, 5, 3, 11, 13, 11, 15, 0, 12, 13, 12),
    (1, None, 6, 7, 7, 1, 5, 6, 9, 5, 6, 8, 8, 9, 10, 11),
    (1, None, 1, 15, 5, 6, 2, 6, 11, 5, 14, 15, 15, 14, 2, 14),
    (12, None, 14, 2, 8, 9, 10, 11, 9, 13, 9, 8, 13, 1, 13, 3),
    (3, None, 1, 2, 8, 6, 2, 11, 12, 10, 6, 10, 13, 1, 15, 3),
)
DIRS = ((1, 0), (-1, 0), (0, 1), (0, -1))


def step(n, dy, dz):
    return (n % 4 + dy) % 4 + ((n // 4 + dz) % 4) * 4


def depth_of(tree, n):
    d = 0
    while PARENT[tree][n] is not None:
        n = PARENT[tree][n]
        d += 1
    return d


DEPTH = tuple(tuple(depth_of(t, n) for n in range(16)) for t in range(8))
CHILD = tuple(
    tuple(tuple(int(PARENT[t][step(n, *d)] == n) for n in range(16)) for d in DIRS) for t in range(8)
)
OFFSET = tuple(tuple(2 * d for d in row) for row in DEPTH)


def pick(n, table):
    value = jnp.int32(table[0])
    for i in range(1, len(table)):
        if table[i] != table[0]:
            value = jnp.where(n == i, jnp.int32(table[i]), value)
    return value


def wrap(v, m):
    return lax.rem(v + m, m)


CH = 32
NCH = 512 // CH
PG = 4
DU = 64
NDU = 256 // DU
ROUNDS = NCH + max(max(o) for o in OFFSET)


class Net:
    def __init__(self, a, pan, rows, diag, m, low, sems):
        self.a, self.pan, self.rows, self.diag, self.m, self.low = a, pan, rows, diag, m, low
        (self.load, self.seed, self.p_send, self.p_recv, self.g_send, self.g_recv, self.q_send, self.q_recv,
         self.d_send, self.d_recv, self.m_send, self.m_recv) = sems
        self.row = lax.axis_index("row")
        self.n = lax.axis_index("col")
        self.x = self.row // 2
        self.core = lax.rem(self.row, 2)
        self.y = lax.rem(self.n, 4)
        self.z = self.n // 4
        self.other = self.at(dcore=1)
        self.depth = [pick(self.n, DEPTH[t]) for t in range(4)]
        self.offset = [pick(self.n, OFFSET[t]) for t in range(8)]
        self.child = [[pick(self.n, CHILD[t][j]) for j in range(4)] for t in range(8)]

    def at(self, dx=0, dcore=0, dy=0, dz=0):
        return (
            wrap(self.x + dx, 4) * 2 + wrap(self.core + dcore, 2),
            wrap(self.z + dz, 4) * 4 + wrap(self.y + dy, 4),
        )

    def remote(self, part, send, recv, dev, src=None):
        return pltpu.make_async_remote_copy(
            part if src is None else src, part, send, recv, dev, device_id_type=MESH
        )

    def barrier(self):
        sem = pltpu.get_barrier_semaphore()
        peers = [dict(dcore=1)]
        peers += [dict(dx=d) for d in (1, 2, 3)] + [dict(dy=d) for d in (1, 2, 3)] + [dict(dz=d) for d in (1, 2, 3)]
        peers += [dict(dcore=1, dy=1), dict(dcore=1, dy=-1)]
        for p in peers:
            pl.semaphore_signal(sem, inc=1, device_id=self.at(**p), device_id_type=MESH)
        pl.semaphore_wait(sem, len(peers))

    def panel_load(self, k, c, t, h):
        return pltpu.make_async_copy(
            self.a.at[pl.ds(t * NCH, NCH), :, 4 * h, :],
            self.pan.at[k, t, :, c, :, pl.ds(h * 128, 128)],
            self.load.at[t, h],
        )

    def row_load(self, k):
        return pltpu.make_async_copy(self.a.at[pl.ds(0, 256 // CH)], self.rows.at[:, k], self.load.at[4, 0])

    def each_own(self, f):
        for k in range(2):
            for c in range(2):
                pl.when((self.n == k) & (self.core == c))(functools.partial(f, k, c))

    def start_loads(self):
        def panel(k, c):
            for t in range(4):
                for h in range(2):
                    self.panel_load(k, c, t, h).start()

        self.each_own(panel)
        for k in range(2):
            @pl.when(self.row == k)
            def _(k=k):
                self.row_load(k).start()

    def seed_copy(self, k, t):
        part = self.pan.at[k, t, :, 0]
        return self.remote(part, self.seed.at[t], self.g_recv.at[4 * k + t, 0], self.other)

    def d_part(self, u):
        return self.diag.at[u]

    def d_own(self, u):
        per = DU // CH
        return self.pan.at[1 if u // NDU == 2 else 0, 0, pl.ds((u % NDU) * per, per), 0 if u // NDU == 0 else 1]

    def wait_load(self, k, c, t):
        for h in range(2):
            self.panel_load(k, c, t, h).wait()

    def own_first(self):
        def panel(k, c):
            self.wait_load(k, c, 0)
            for d in range(3):
                if (c, k) == ((0, 0), (1, 0), (1, 1))[d]:
                    @pl.when(self.x == 0)
                    def _(d=d):
                        for u in range(d * NDU, d * NDU + NDU):
                            if d == 0:
                                pltpu.make_async_copy(self.d_own(u), self.d_part(u), self.d_recv.at[u]).start()
                            else:
                                self.d_seed(u).start()

        self.each_own(panel)

    def own_rest(self):
        def panel(k, c):
            for t in range(4):
                if t > 0:
                    self.wait_load(k, c, t)
                if c == 0:
                    self.seed_copy(k, t).start()

        self.each_own(panel)
        @pl.when(self.row == 0)
        def _():
            self.row_load(0).wait()

        @pl.when(self.row == 1)
        def _():
            self.row_load(1).wait()
            self.row_copy().start()

    def row_copy(self):
        part = self.rows.at[:, 1]
        return self.remote(part, self.q_send.at[8], self.q_recv.at[8], self.other)

    def d_seed(self, u):
        return self.remote(self.d_part(u), self.d_send.at[u, 9], self.d_recv.at[u], (0, 0), self.d_own(u))

    def d_copy(self, u, j, dev):
        return self.remote(self.d_part(u), self.d_send.at[u, j], self.d_recv.at[u], dev)

    def d_each(self, t, d, f, tree=True, line=True):
        u = d * NDU + t
        if tree:
            for j, (dy, dz) in enumerate(DIRS):
                @pl.when(self.child[t][j] == 1)
                def _(j=j, dy=dy, dz=dz):
                    f(self.d_copy(u, j, self.at(dy=dy, dz=dz)))
        if line:
            for j, dx in enumerate((1, 3, 2)):
                f(self.d_copy(u, 4 + j, self.at(dx=dx)))

    def d_source(self):
        for d in range(3):
            for t in range(NDU):
                self.d_copy(d * NDU + t, 0, self.other).wait_recv()
                self.d_each(t, d, lambda c: c.start(), line=False)

    def d_line(self):
        for d in range(3):
            for t in range(NDU):
                self.d_each(t, d, lambda c: c.start(), tree=False)

    def d_wait(self, d):
        for t in range(NDU):
            self.d_copy(d * NDU + t, 0, self.other).wait_recv()

    def d_spread(self):
        def one(i, _):
            for t in range(NDU):
                d = i - self.depth[t]

                @pl.when((d >= 0) & (d < 3))
                def _(t=t, d=d):
                    self.d_copy(d * NDU + t, 0, self.other).wait_recv()
                    self.d_each(t, d, lambda c: c.start())

            return 0

        lax.fori_loop(0, 3 + max(max(DEPTH[t]) for t in range(4)), one, 0)

    def d_drain(self):
        def one(d, _):
            for t in range(NDU):
                self.d_each(t, d, lambda c: c.wait_send())
            return 0

        lax.fori_loop(0, 3, one, 0)

    def q_copy(self, u, dev):
        return self.remote(self.rows.at[u], self.q_send.at[u], self.q_recv.at[u], dev)

    def q_on(self, half):
        return (self.x != 3) if half == 0 else (self.x != 1)

    def q_dev(self, half):
        return self.at(dx=1 if half == 0 else -1)

    def q_first(self):
        self.row_copy().wait_recv()
        for c in range(4):
            for half in range(2):
                self.q_copy(half * 4 + c, self.q_dev(half)).start()

    def q_spread(self):
        def one(i, _):
            for half in range(2):
                c = i - (self.x - 1 if half == 0 else 3 - self.x)

                @pl.when((c >= 0) & (c < 4) & self.q_on(half))
                def _(half=half, c=c):
                    u = half * 4 + c
                    self.q_copy(u, self.other).wait_recv()
                    self.q_copy(u, self.q_dev(half)).start()

            return 0

        lax.fori_loop(0, 5, one, 0)

    def q_last(self):
        for half in range(2):
            @pl.when(jnp.logical_not(self.q_on(half)))
            def _(half=half):
                for c in range(4):
                    self.q_copy(half * 4 + c, self.other).wait_recv()

    def q_drain(self):
        for half in range(2):
            @pl.when(self.q_on(half))
            def _(half=half):
                for c in range(4):
                    self.q_copy(half * 4 + c, self.q_dev(half)).wait_send()

    def p_copy(self, t, q, j):
        dy, dz = DIRS[j]
        return self.remote(
            self.pan.at[t // 4, t % 4, q], self.p_send.at[t, j, q], self.p_recv.at[t, q], self.at(dy=dy, dz=dz)
        )

    def p_group(self, t, g):
        part = self.pan.at[t // 4, lax.rem(t, 4), pl.ds(g * PG, PG), 0]
        return self.remote(part, self.g_send.at[t, g], self.g_recv.at[t, g], self.other)

    def is_root(self, t):
        return self.n == t // 4

    def p_start(self):
        for k in range(2):
            @pl.when(self.n == k)
            def _(k=k):
                for t in range(4):
                    self.seed_copy(k, t).wait_recv()

    def p_round(self, i):
        for t in range(8):
            q = i - self.offset[t]

            @pl.when((q >= 0) & (q < NCH))
            def _(t=t, q=q):
                root = self.is_root(t)

                @pl.when(jnp.logical_not(root))
                def _():
                    self.p_copy(t, q, 0).wait_recv()

                for j in range(4):
                    @pl.when(self.child[t][j] == 1)
                    def _(j=j):
                        self.p_copy(t, q, j).start()

                @pl.when(jnp.logical_not(root) & (lax.rem(q, PG) == PG - 1))
                def _():
                    self.p_group(t, q // PG).start()

    def p_drain(self):
        for t in range(8):
            for j in range(4):
                @pl.when(self.child[t][j] == 1)
                def _(t=t, j=j):
                    def one(q, _):
                        self.p_copy(t, q, j).wait_send()
                        return 0
                    lax.fori_loop(0, NCH, one, 0)

            @pl.when(jnp.logical_not(self.is_root(t)))
            def _(t=t):
                for g in range(NCH // PG):
                    self.p_group(t, g).wait_send()

    def p_land(self, t):
        for k in range(2):
            @pl.when(self.n != k)
            def _(k=k):
                for g in range(NCH // PG):
                    self.p_group(4 * k + t, g).wait_recv()

    def own_drain(self):
        def panel(k, c):
            for d in (1, 2):
                if (c, k) == (1, d - 1):
                    @pl.when(self.x == 0)
                    def _(d=d):
                        for u in range(d * NDU, d * NDU + NDU):
                            self.d_seed(u).wait_send()
            if c == 0:
                for t in range(4):
                    self.seed_copy(k, t).wait_send()

        self.each_own(panel)

        @pl.when(self.row == 1)
        def _():
            self.row_copy().wait_send()

    def m_copy(self, i):
        return self.remote(self.m.at[i], self.m_send.at[i], self.m_recv.at[i], self.other)

    def low_copy(self):
        return self.remote(self.low.at[1], self.m_send.at[2], self.m_recv.at[2], self.other)


SEMS = (
    pltpu.SemaphoreType.DMA((5, 2)),
    pltpu.SemaphoreType.DMA((4,)),
    pltpu.SemaphoreType.DMA((8, 4, NCH)),
    pltpu.SemaphoreType.DMA((8, NCH)),
    pltpu.SemaphoreType.DMA((8, NCH // PG)),
    pltpu.SemaphoreType.DMA((8, NCH // PG)),
    pltpu.SemaphoreType.DMA((9,)),
    pltpu.SemaphoreType.DMA((9,)),
    pltpu.SemaphoreType.DMA((3 * NDU, 10)),
    pltpu.SemaphoreType.DMA((3 * NDU,)),
    pltpu.SemaphoreType.DMA((3,)),
    pltpu.SemaphoreType.DMA((3,)),
)


def split(x):
    hi = x.astype(BF16)
    return hi, (x - hi.astype(F32)).astype(BF16)


def mm(a, b, ta=False, precision=None):
    return lax.dot_general(
        a, b, (((0 if ta else 1,), (0,)), ((), ())), preferred_element_type=F32, precision=precision
    )


def mm3(a, b, ta=False):
    (ah, al), (bh, bl) = a, b
    return mm(ah, bh, ta) + (mm(ah, bl, ta) + mm(al, bh, ta))


def factor128(xa, xi, ta, ti):
    sub = lax.broadcasted_iota(jnp.int32, (8, 128), 0)

    def row(v, p):
        return jnp.broadcast_to(v[p : p + 1, :], (8, 128))

    def lane(v, c):
        return jnp.broadcast_to(v[:, c : c + 1], (8, 128))

    def total(s):
        return ((s[0] + s[1]) + (s[2] + s[3])) + ((s[4] + s[5]) + (s[6] + s[7]))

    first = xa[0:8, :]
    col = [lane(first, k) for k in range(8)]
    for j in range(16):
        here = pl.ds(8 * j, 8)
        ra, ri = xa[here, :], xi[here, :]
        last = j == 15
        if not last:
            nxt = xa[pl.ds(8 * j + 8, 8), :]
            b = [lane(nxt, 8 * j + k) for k in range(8)]
            ahead = [lane(nxt, 8 * j + 8 + k) for k in range(8)]
            below = list(b)
        la = jnp.zeros((8, 128), F32)
        li, rd = la, la
        for p in range(8):
            d = row(col[p], p)
            inv, root = 1.0 / d, lax.rsqrt(d)
            m = jnp.where(sub == p, 0.0, col[p] * inv)
            pa, pi = row(ra, p), row(ri, p)
            if p < 7:
                head = [row(col[k], p) for k in range(p + 1, 8)]
                for k in range(p + 1, 8):
                    col[k] = col[k] - m * head[k - p - 1]
            if not last:
                mb = b[p] * inv
                for k in range(p + 1, 8):
                    b[k] = b[k] - mb * head[k - p - 1]
                for k in range(8):
                    ahead[k] = ahead[k] - mb * row(b[p], k)
            la = jnp.where(sub == p, pa * root, la)
            li = jnp.where(sub == p, pi * root, li)
            rd = jnp.where(sub == p, inv, rd)
            ra, ri = ra - m * pa, ri - m * pi
        ta[here, :], ti[here, :] = la, li
        if not last:
            va, vi = ra * rd, ri * rd
            va = [row(va, k) for k in range(8)]
            vi = [row(vi, k) for k in range(8)]
            for g in range(j + 1, 16):
                there = pl.ds(8 * g, 8)
                xg = xa[there, :]
                c = below if g == j + 1 else [lane(xg, 8 * j + k) for k in range(8)]
                xa[there, :] = xg - total([c[k] * va[k] for k in range(8)])
                xi[there, :] = xi[there, :] - total([c[k] * vi[k] for k in range(8)])
            col = ahead


def factor512(s, w, xa, xi, ta, ti, join):
    w[...] = jnp.zeros((512, 512), F32)
    i0 = lax.broadcasted_iota(jnp.int32, (128, 128), 0)
    i1 = lax.broadcasted_iota(jnp.int32, (128, 128), 1)

    def body(b, _):
        here = pl.ds(pl.multiple_of(b * 128, 128), 128)
        xa[...] = s[here, here]
        xi[...] = jnp.where(i0 == i1, 1.0, 0.0).astype(F32)
        factor128(xa, xi, ta, ti)
        w[here, here] = ti[...]
        s[here, here] = jnp.where(i1 >= i0, ta[...], 0.0)
        for bb in range(4):
            @pl.when(b == bb)
            def _(bb=bb):
                n0, n1 = bb * 128, bb * 128 + 128
                r, rest = pl.ds(n0, 128), pl.ds(n1, 128)
                inv = ti[...]
                if bb > 0:
                    w[r, 0:n0] = mm(inv, w[r, 0:n0], precision=HIGHEST)
                if bb % 2 == 0:
                    u = mm(inv, s[r, rest], precision=HIGHEST)
                    s[r, rest] = u
                    s[rest, rest] = s[rest, rest] - mm(u, u, True, HIGHEST)
                    w[rest, 0:n1] = w[rest, 0:n1] - mm(u, w[r, 0:n1], True, HIGHEST)
                if bb == 1:
                    below, corner = join()
                    first = w[0:256, 0:256]
                    u = mm(first, below.T, precision=HIGHEST)
                    s[256:512, 256:512] = symmetrise(corner) - mm(u, u, True, HIGHEST)
                    w[256:512, 0:256] = -mm(u, first, True, HIGHEST)
        return 0

    lax.fori_loop(0, 4, body, 0)


def transposed_upper(s):
    i0 = lax.broadcasted_iota(jnp.int32, (256, 256), 0)
    i1 = lax.broadcasted_iota(jnp.int32, (256, 256), 1)
    return jnp.where(i1 >= i0, s, 0.0).T


def symmetrise(x):
    return (x + x.T) * 0.5


def block(diag, d):
    return diag[d * NDU : d * NDU + NDU].reshape(256, 256)


def gather_rows(rows, rh, rl):
    flat = rows.reshape(8 * 2 * CH * 8, 128)
    for k in range(2):
        for u in range(8):
            r = pl.ds(k * 256 + u * CH, CH)
            for q in range(8):
                hi, lo = split(flat[pl.ds((u * 2 + k) * CH * 8 + q, CH, stride=8), :])
                rh[r, q * 128 : q * 128 + 128] = hi
                rl[r, q * 128 : q * 128 + 128] = lo


def solve_rows(w, n, rh, rl, m, done):
    w00, w10, w11 = split(w[0:256, 0:256]), split(w[256:512, 0:256]), split(w[256:512, 256:512])
    for half in range(2):
        cols = pl.ds(half * 512, 512)
        r0, r1 = (rh[0:256, cols], rl[0:256, cols]), (rh[256:512, cols], rl[256:512, cols])
        t0 = split(mm3(w00, r0))
        t1 = split(mm3(w10, r0) + mm3(w11, r1))
        m[half, 0:256] = mm3(w00, t0, True) + mm3(w10, t1, True)
        m[half, 256:512] = mm3(w11, t1, True)
        for k in range(2):
            @pl.when(n == k)
            def _(k=k):
                m[half, :, 0:128] = -w[pl.ds(k * 256 + half * 128, 128), :].T
        done(half)


def update_tile(out, pan, m, core, t, half, keep):
    o2 = out.reshape(2048 * 8, 128)
    left = [split(pan[k, t, :, core].reshape(512, 256)) for k in range(2)]
    right = [split(m[half, k * 256 : k * 256 + 256]) for k in range(2)]
    prod = mm3(left[0], right[0]) + mm3(left[1], right[1])
    for q in range(4):
        there = pl.ds(t * 512 * 8 + half * 4 + q, 512, stride=8)
        held = o2[there, :]
        if q == 0:
            held = held * keep
        o2[there, :] = held - prod[:, q * 128 : q * 128 + 128]


def own_rows(out, low, row, n):
    o2 = out.reshape(2048 * 8, 128)
    for q in range(8):
        there = pl.ds(q, 256, stride=8)
        if q % 4:
            o2[there, :] = jnp.zeros((256, 128), F32)
        else:
            h = (q // 4) * 128
            own = jnp.where(n == 0, low[0, :, h : h + 128], low[1, :, h : h + 128])
            o2[there, :] = jnp.where(row == n, own, jnp.where((row == 1) & (n == 0), o2[there, :], 0.0))


def kernel(a, out, pan, rows, diag, s, w, low, xa, xi, ta, ti, rh, rl, m, a_sem, *sems):
    net = Net(a, pan, rows, diag, m, low, sems)
    net.start_loads()
    held = pltpu.make_async_copy(a, out, a_sem)
    net.barrier()
    net.own_first()
    held.start()
    source = (net.row == 0) & (net.n == 0)
    pl.when(source)(net.d_source)
    net.own_rest()
    keep = jnp.where(net.n < 2, 0.0, 1.0).astype(F32)

    @pl.when(net.core == 0)
    def _():
        @pl.when(net.x == 0)
        def _():
            net.q_first()
            pl.when(source)(net.d_line)
            pl.when(net.n != 0)(net.d_spread)
            gather_rows(rows, rh, rl)

        pl.when(net.x != 0)(net.q_spread)
        pl.when(net.x != 0)(lambda: net.d_wait(0))
        s[0:256, 0:256] = symmetrise(block(diag, 0))

        def join():
            @pl.when(net.x != 0)
            def _():
                net.q_last()
                gather_rows(rows, rh, rl)
                net.d_wait(1)
                net.d_wait(2)

            return block(diag, 1), block(diag, 2)


        factor512(s, w, xa, xi, ta, ti, join)
        solve_rows(w, net.n, rh, rl, m, lambda i: net.m_copy(i).start())
        low[0] = transposed_upper(s[0:256, 0:256])
        low[1] = transposed_upper(s[256:512, 256:512])
        net.low_copy().start()

    @pl.when(net.core == 1)
    def _():
        low[0] = jnp.zeros((256, 256), F32)
        net.p_start()

        def one(i, _):
            net.p_round(i)
            return 0

        lax.fori_loop(0, ROUNDS, one, 0)
        for i in range(2):
            net.m_copy(i).wait_recv()

    held.wait()

    def tile(t, _):
        pl.when(net.core == 0)(lambda: net.p_land(t))
        for half in range(2):
            update_tile(out, pan, m, net.core, t, half, keep)
        return 0

    lax.fori_loop(0, 4, tile, 0)

    @pl.when(net.core == 1)
    def _():
        net.low_copy().wait_recv()

    @pl.when(net.row < 2)
    def _():
        own_rows(out, low, net.row, net.n)

    @pl.when(net.core == 0)
    def _():
        pl.when(net.x == 0)(net.d_drain)
        net.q_drain()
        for i in range(2):
            net.m_copy(i).wait_send()
        net.low_copy().wait_send()

    @pl.when(net.core == 1)
    def _():
        net.p_drain()

    net.own_drain()


def two_steps(a):
    return pl.pallas_call(
        kernel,
        out_shape=pltpu.VMEM(a.shape, F32),
        in_specs=[pl.BlockSpec(memory_space=pl.ANY)],
        out_specs=pl.BlockSpec(memory_space=pltpu.VMEM),
        scratch_shapes=[
            pltpu.VMEM((2, 4, NCH, 2, CH, 256), F32),
            pltpu.VMEM((8, 2, CH, 8, 128), F32),
            pltpu.VMEM((3 * NDU, DU // CH, CH, 256), F32),
            pltpu.VMEM((512, 512), F32),
            pltpu.VMEM((512, 512), F32),
            pltpu.VMEM((2, 256, 256), F32),
        ]
        + [pltpu.VMEM((128, 128), F32)] * 4
        + [pltpu.VMEM((512, 1024), BF16)] * 2
        + [pltpu.VMEM((2, 512, 512), F32), pltpu.SemaphoreType.DMA]
        + list(SEMS),
        compiler_params=pltpu.CompilerParams(
            collective_id=0, has_side_effects=True, vmem_limit_bytes=46 * 2**20
        ),
        name="steps",
    )(a)


def shards(covariance):
    a = covariance.reshape(8, 256, 4, 2, 128).transpose(0, 1, 3, 2, 4).reshape(2048 // CH, CH, 8, 128)
    out = two_steps(a)
    return out.reshape(8, 256, 2, 4, 128).transpose(0, 1, 3, 2, 4).reshape(covariance.shape)


def solution(mesh):
    spec = P("row", None, None, "col", None, None)
    return jax.shard_map(shards, mesh=mesh, in_specs=(spec,), out_specs=spec, check_vma=False)
```

```python
import functools

import jax
import jax.numpy as jnp
from jax import lax
from jax.experimental import pallas as pl
from jax.experimental.pallas import tpu as pltpu
from jax.sharding import PartitionSpec as P

F32 = jnp.float32
BF16 = jnp.bfloat16
HIGHEST = lax.Precision.HIGHEST
MESH = pl.DeviceIdType.MESH

PARENT = (
    (None, 5, 3, 0, 0, 4, 10, 4, 4, 10, 14, 10, 15, 14, 2, 14),
    (None, 2, 3, 0, 5, 9, 7, 3, 12, 8, 11, 7, 0, 9, 10, 11),
    (None, 0, 6, 7, 0, 4, 7, 4, 4, 8, 9, 7, 8, 12, 15, 12),
    (None, 0, 14, 15, 7, 1, 5, 3, 11, 13, 11, 15, 0, 12, 13, 12),
    (1, None, 6, 7, 7, 1, 5, 6, 9, 5, 6, 8, 8, 9, 10, 11),
    (1, None, 1, 15, 5, 6, 2, 6, 11, 5, 14, 15, 15, 14, 2, 14),
    (12, None, 14, 2, 8, 9, 10, 11, 9, 13, 9, 8, 13, 1, 13, 3),
    (3, None, 1, 2, 8, 6, 2, 11, 12, 10, 6, 10, 13, 1, 15, 3),
)
DIRS = ((1, 0), (-1, 0), (0, 1), (0, -1))


def step(n, dy, dz):
    return (n % 4 + dy) % 4 + ((n // 4 + dz) % 4) * 4


def depth_of(tree, n):
    d = 0
    while PARENT[tree][n] is not None:
        n = PARENT[tree][n]
        d += 1
    return d


DEPTH = tuple(tuple(depth_of(t, n) for n in range(16)) for t in range(8))
CHILD = tuple(
    tuple(tuple(int(PARENT[t][step(n, *d)] == n) for n in range(16)) for d in DIRS) for t in range(8)
)
OFFSET = tuple(tuple(5 * d // 2 for d in row) for row in DEPTH)


def pick(n, table):
    value = jnp.int32(table[0])
    for i in range(1, len(table)):
        if table[i] != table[0]:
            value = jnp.where(n == i, jnp.int32(table[i]), value)
    return value


def wrap(v, m):
    return lax.rem(v + m, m)


CH = 32
NCH = 512 // CH
PG = 8
NG = NCH // PG
FIRST = 256 // CH // PG
DU = 64
NDU = 256 // DU
ROUNDS = NCH + max(max(o) for o in OFFSET)


class Net:
    def __init__(self, a, pan, rows, diag, m, low, sems):
        self.a, self.pan, self.rows, self.diag, self.m, self.low = a, pan, rows, diag, m, low
        (self.load, self.seed, self.p_send, self.p_recv, self.g_send, self.g_recv, self.q_send, self.q_recv,
         self.d_send, self.d_recv, self.m_send, self.m_recv) = sems
        self.row = lax.axis_index("row")
        self.n = lax.axis_index("col")
        self.x = self.row // 2
        self.core = lax.rem(self.row, 2)
        self.y = lax.rem(self.n, 4)
        self.z = self.n // 4
        self.other = self.at(dcore=1)
        self.depth = [pick(self.n, DEPTH[t]) for t in range(4)]
        self.offset = [pick(self.n, OFFSET[t]) for t in range(8)]
        self.child = [[pick(self.n, CHILD[t][j]) for j in range(4)] for t in range(8)]

    def at(self, dx=0, dcore=0, dy=0, dz=0):
        return (
            wrap(self.x + dx, 4) * 2 + wrap(self.core + dcore, 2),
            wrap(self.z + dz, 4) * 4 + wrap(self.y + dy, 4),
        )

    def remote(self, part, send, recv, dev, src=None):
        return pltpu.make_async_remote_copy(
            part if src is None else src, part, send, recv, dev, device_id_type=MESH
        )

    def barrier(self):
        sem = pltpu.get_barrier_semaphore()
        peers = [dict(dcore=1)]
        peers += [dict(dx=d) for d in (1, 2, 3)] + [dict(dy=d) for d in (1, 2, 3)] + [dict(dz=d) for d in (1, 2, 3)]
        peers += [dict(dcore=1, dy=1), dict(dcore=1, dy=-1)]
        for p in peers:
            pl.semaphore_signal(sem, inc=1, device_id=self.at(**p), device_id_type=MESH)
        pl.semaphore_wait(sem, len(peers))

    def panel_load(self, k, c, t, g, h):
        return pltpu.make_async_copy(
            self.a.at[pl.ds(t * NCH + g * PG, PG), :, 4 * h, :],
            self.pan.at[k, t, pl.ds(g * PG, PG), c, :, pl.ds(h * 128, 128)],
            self.load.at[t, g, h],
        )

    def row_load(self, k):
        return pltpu.make_async_copy(self.a.at[pl.ds(0, 256 // CH)], self.rows.at[:, k], self.load.at[4, 0, 0])

    def each_own(self, f):
        for k in range(2):
            for c in range(2):
                pl.when((self.n == k) & (self.core == c))(functools.partial(f, k, c))

    def start_loads(self):
        def panel(k, c):
            for g in range(NG):
                for t in range(4):
                    for h in range(2):
                        self.panel_load(k, c, t, g, h).start()

        self.each_own(panel)
        for k in range(2):
            @pl.when(self.row == k)
            def _(k=k):
                self.row_load(k).start()

    def seed_copy(self, k, t, g):
        part = self.pan.at[k, t, pl.ds(g * PG, PG), 0]
        return self.remote(part, self.seed.at[t, g], self.g_recv.at[4 * k + t, g], self.other)

    def d_part(self, u):
        return self.diag.at[u]

    def d_own(self, u):
        per = DU // CH
        return self.pan.at[1 if u // NDU == 2 else 0, 0, pl.ds((u % NDU) * per, per), 0 if u // NDU == 0 else 1]

    def wait_load(self, k, c, t, g):
        for h in range(2):
            self.panel_load(k, c, t, g, h).wait()

    def own_first(self):
        def panel(k, c):
            for g in range(FIRST):
                self.wait_load(k, c, 0, g)
            for d in range(3):
                if (c, k) == ((0, 0), (1, 0), (1, 1))[d]:
                    @pl.when(self.x == 0)
                    def _(d=d):
                        for u in range(d * NDU, d * NDU + NDU):
                            if d == 0:
                                pltpu.make_async_copy(self.d_own(u), self.d_part(u), self.d_recv.at[u]).start()
                            else:
                                self.d_seed(u).start()

        self.each_own(panel)

    def own_rest(self):
        def panel(k, c):
            if c == 0:
                for g in range(NG):
                    for t in range(4):
                        if t > 0 or g >= FIRST:
                            self.wait_load(k, c, t, g)
                        self.seed_copy(k, t, g).start()

        self.each_own(panel)
        @pl.when(self.row == 0)
        def _():
            self.row_load(0).wait()

        @pl.when(self.row == 1)
        def _():
            self.row_load(1).wait()
            self.row_copy().start()

    def row_copy(self):
        part = self.rows.at[:, 1]
        return self.remote(part, self.q_send.at[8], self.q_recv.at[8], self.other)

    def d_seed(self, u):
        return self.remote(self.d_part(u), self.d_send.at[u, 9], self.d_recv.at[u], (0, 0), self.d_own(u))

    def d_copy(self, u, j, dev):
        return self.remote(self.d_part(u), self.d_send.at[u, j], self.d_recv.at[u], dev)

    def d_each(self, t, d, f, tree=True, line=True):
        u = d * NDU + t
        if tree:
            for j, (dy, dz) in enumerate(DIRS):
                @pl.when(self.child[t][j] == 1)
                def _(j=j, dy=dy, dz=dz):
                    f(self.d_copy(u, j, self.at(dy=dy, dz=dz)))
        if line:
            for j, dx in enumerate((1, 3, 2)):
                f(self.d_copy(u, 4 + j, self.at(dx=dx)))

    def d_source(self):
        for d in range(3):
            for t in range(NDU):
                self.d_copy(d * NDU + t, 0, self.other).wait_recv()
                self.d_each(t, d, lambda c: c.start(), line=False)

    def d_line(self):
        for d in range(3):
            for t in range(NDU):
                self.d_each(t, d, lambda c: c.start(), tree=False)

    def d_wait(self, d):
        for t in range(NDU):
            self.d_copy(d * NDU + t, 0, self.other).wait_recv()

    def d_spread(self):
        def one(i, _):
            for t in range(NDU):
                d = i - self.depth[t]

                @pl.when((d >= 0) & (d < 3))
                def _(t=t, d=d):
                    self.d_copy(d * NDU + t, 0, self.other).wait_recv()
                    self.d_each(t, d, lambda c: c.start())

            return 0

        lax.fori_loop(0, 3 + max(max(DEPTH[t]) for t in range(4)), one, 0)

    def d_drain(self):
        def one(d, _):
            for t in range(NDU):
                self.d_each(t, d, lambda c: c.wait_send())
            return 0

        lax.fori_loop(0, 3, one, 0)

    def q_copy(self, u, dev):
        return self.remote(self.rows.at[u], self.q_send.at[u], self.q_recv.at[u], dev)

    def q_on(self, half):
        return (self.x != 3) if half == 0 else (self.x != 1)

    def q_dev(self, half):
        return self.at(dx=1 if half == 0 else -1)

    def q_first(self):
        self.row_copy().wait_recv()
        for c in range(4):
            for half in range(2):
                self.q_copy(half * 4 + c, self.q_dev(half)).start()

    def q_spread(self):
        def one(i, _):
            for half in range(2):
                c = i - (self.x - 1 if half == 0 else 3 - self.x)

                @pl.when((c >= 0) & (c < 4) & self.q_on(half))
                def _(half=half, c=c):
                    u = half * 4 + c
                    self.q_copy(u, self.other).wait_recv()
                    self.q_copy(u, self.q_dev(half)).start()

            return 0

        lax.fori_loop(0, 5, one, 0)

    def q_last(self):
        for half in range(2):
            @pl.when(jnp.logical_not(self.q_on(half)))
            def _(half=half):
                for c in range(4):
                    self.q_copy(half * 4 + c, self.other).wait_recv()

    def q_drain(self):
        for half in range(2):
            @pl.when(self.q_on(half))
            def _(half=half):
                for c in range(4):
                    self.q_copy(half * 4 + c, self.q_dev(half)).wait_send()

    def p_copy(self, t, q, j):
        dy, dz = DIRS[j]
        return self.remote(
            self.pan.at[t // 4, t % 4, q], self.p_send.at[t, j, q], self.p_recv.at[t, q], self.at(dy=dy, dz=dz)
        )

    def p_group(self, t, g):
        part = self.pan.at[t // 4, lax.rem(t, 4), pl.ds(g * PG, PG), 0]
        return self.remote(part, self.g_send.at[t, g], self.g_recv.at[t, g], self.other)

    def is_root(self, t):
        return self.n == t // 4

    def p_ready(self, t, g):
        k = t // 4
        if t % 4 == 0:
            @pl.when(g >= FIRST)
            def _():
                self.wait_load(k, 1, t % 4, g)
        else:
            self.wait_load(k, 1, t % 4, g)
        self.seed_copy(k, t % 4, g).wait_recv()

    def p_round(self, i):
        for t in range(8):
            q = i - self.offset[t]

            @pl.when((q >= 0) & (q < NCH))
            def _(t=t, q=q):
                root = self.is_root(t)

                @pl.when(jnp.logical_not(root))
                def _():
                    self.p_copy(t, q, 0).wait_recv()

                @pl.when(root & (lax.rem(q, PG) == 0))
                def _():
                    self.p_ready(t, q // PG)

                for j in range(4):
                    @pl.when(self.child[t][j] == 1)
                    def _(j=j):
                        self.p_copy(t, q, j).start()

                @pl.when(jnp.logical_not(root) & (lax.rem(q, PG) == PG - 1))
                def _():
                    self.p_group(t, q // PG).start()

    def p_drain(self):
        for t in range(8):
            for j in range(4):
                @pl.when(self.child[t][j] == 1)
                def _(t=t, j=j):
                    def one(q, _):
                        self.p_copy(t, q, j).wait_send()
                        return 0
                    lax.fori_loop(0, NCH, one, 0)

            @pl.when(jnp.logical_not(self.is_root(t)))
            def _(t=t):
                for g in range(NCH // PG):
                    self.p_group(t, g).wait_send()

    def p_land(self, t):
        for k in range(2):
            @pl.when(self.n != k)
            def _(k=k):
                for g in range(NCH // PG):
                    self.p_group(4 * k + t, g).wait_recv()

    def own_drain(self):
        def panel(k, c):
            for d in (1, 2):
                if (c, k) == (1, d - 1):
                    @pl.when(self.x == 0)
                    def _(d=d):
                        for u in range(d * NDU, d * NDU + NDU):
                            self.d_seed(u).wait_send()
            if c == 0:
                for t in range(4):
                    for g in range(NG):
                        self.seed_copy(k, t, g).wait_send()

        self.each_own(panel)

        @pl.when(self.row == 1)
        def _():
            self.row_copy().wait_send()

    def m_copy(self, i):
        return self.remote(self.m.at[i], self.m_send.at[i], self.m_recv.at[i], self.other)

    def low_copy(self):
        return self.remote(self.low.at[1], self.m_send.at[2], self.m_recv.at[2], self.other)


SEMS = (
    pltpu.SemaphoreType.DMA((5, NG, 2)),
    pltpu.SemaphoreType.DMA((4, NG)),
    pltpu.SemaphoreType.DMA((8, 4, NCH)),
    pltpu.SemaphoreType.DMA((8, NCH)),
    pltpu.SemaphoreType.DMA((8, NCH // PG)),
    pltpu.SemaphoreType.DMA((8, NCH // PG)),
    pltpu.SemaphoreType.DMA((9,)),
    pltpu.SemaphoreType.DMA((9,)),
    pltpu.SemaphoreType.DMA((3 * NDU, 10)),
    pltpu.SemaphoreType.DMA((3 * NDU,)),
    pltpu.SemaphoreType.DMA((3,)),
    pltpu.SemaphoreType.DMA((3,)),
)


def split(x):
    hi = x.astype(BF16)
    return hi, (x - hi.astype(F32)).astype(BF16)


def mm(a, b, ta=False, precision=None):
    return lax.dot_general(
        a, b, (((0 if ta else 1,), (0,)), ((), ())), preferred_element_type=F32, precision=precision
    )


def mm3(a, b, ta=False):
    (ah, al), (bh, bl) = a, b
    return mm(ah, bh, ta) + (mm(ah, bl, ta) + mm(al, bh, ta))


def factor128(xa, xi, ta, ti):
    sub = lax.broadcasted_iota(jnp.int32, (8, 128), 0)

    def row(v, p):
        return jnp.broadcast_to(v[p : p + 1, :], (8, 128))

    def lane(v, c):
        return jnp.broadcast_to(v[:, c : c + 1], (8, 128))

    def total(s):
        return ((s[0] + s[1]) + (s[2] + s[3])) + ((s[4] + s[5]) + (s[6] + s[7]))

    first = xa[0:8, :]
    col = [lane(first, k) for k in range(8)]
    for j in range(16):
        here = pl.ds(8 * j, 8)
        ra, ri = xa[here, :], xi[here, :]
        last = j == 15
        if not last:
            nxt = xa[pl.ds(8 * j + 8, 8), :]
            b = [lane(nxt, 8 * j + k) for k in range(8)]
            ahead = [lane(nxt, 8 * j + 8 + k) for k in range(8)]
            below = list(b)
        la = jnp.zeros((8, 128), F32)
        li, rd = la, la
        for p in range(8):
            d = row(col[p], p)
            inv, root = 1.0 / d, lax.rsqrt(d)
            m = jnp.where(sub == p, 0.0, col[p] * inv)
            pa, pi = row(ra, p), row(ri, p)
            if p < 7:
                head = [row(col[k], p) for k in range(p + 1, 8)]
                for k in range(p + 1, 8):
                    col[k] = col[k] - m * head[k - p - 1]
            if not last:
                mb = b[p] * inv
                for k in range(p + 1, 8):
                    b[k] = b[k] - mb * head[k - p - 1]
                for k in range(8):
                    ahead[k] = ahead[k] - mb * row(b[p], k)
            la = jnp.where(sub == p, pa * root, la)
            li = jnp.where(sub == p, pi * root, li)
            rd = jnp.where(sub == p, inv, rd)
            ra, ri = ra - m * pa, ri - m * pi
        ta[here, :], ti[here, :] = la, li
        if not last:
            va, vi = ra * rd, ri * rd
            va = [row(va, k) for k in range(8)]
            vi = [row(vi, k) for k in range(8)]
            for g in range(j + 1, 16):
                there = pl.ds(8 * g, 8)
                xg = xa[there, :]
                c = below if g == j + 1 else [lane(xg, 8 * j + k) for k in range(8)]
                xa[there, :] = xg - total([c[k] * va[k] for k in range(8)])
                xi[there, :] = xi[there, :] - total([c[k] * vi[k] for k in range(8)])
            col = ahead


def factor512(s, w, xa, xi, ta, ti, join):
    w[...] = jnp.zeros((512, 512), F32)
    i0 = lax.broadcasted_iota(jnp.int32, (128, 128), 0)
    i1 = lax.broadcasted_iota(jnp.int32, (128, 128), 1)

    def body(b, _):
        here = pl.ds(pl.multiple_of(b * 128, 128), 128)
        xa[...] = s[here, here]
        xi[...] = jnp.where(i0 == i1, 1.0, 0.0).astype(F32)
        factor128(xa, xi, ta, ti)
        w[here, here] = ti[...]
        s[here, here] = jnp.where(i1 >= i0, ta[...], 0.0)
        for bb in range(4):
            @pl.when(b == bb)
            def _(bb=bb):
                n0, n1 = bb * 128, bb * 128 + 128
                r, rest = pl.ds(n0, 128), pl.ds(n1, 128)
                inv = ti[...]
                if bb > 0:
                    w[r, 0:n0] = mm(inv, w[r, 0:n0], precision=HIGHEST)
                if bb % 2 == 0:
                    u = mm(inv, s[r, rest], precision=HIGHEST)
                    s[r, rest] = u
                    s[rest, rest] = s[rest, rest] - mm(u, u, True, HIGHEST)
                    w[rest, 0:n1] = w[rest, 0:n1] - mm(u, w[r, 0:n1], True, HIGHEST)
                if bb == 1:
                    below, corner = join()
                    first = w[0:256, 0:256]
                    u = mm(first, below.T, precision=HIGHEST)
                    s[256:512, 256:512] = symmetrise(corner) - mm(u, u, True, HIGHEST)
                    w[256:512, 0:256] = -mm(u, first, True, HIGHEST)
        return 0

    lax.fori_loop(0, 4, body, 0)


def transposed_upper(s):
    i0 = lax.broadcasted_iota(jnp.int32, (256, 256), 0)
    i1 = lax.broadcasted_iota(jnp.int32, (256, 256), 1)
    return jnp.where(i1 >= i0, s, 0.0).T


def symmetrise(x):
    return (x + x.T) * 0.5


def block(diag, d):
    return diag[d * NDU : d * NDU + NDU].reshape(256, 256)


def gather_rows(rows, rh, rl):
    flat = rows.reshape(8 * 2 * CH * 8, 128)
    for k in range(2):
        for u in range(8):
            r = pl.ds(k * 256 + u * CH, CH)
            for q in range(8):
                hi, lo = split(flat[pl.ds((u * 2 + k) * CH * 8 + q, CH, stride=8), :])
                rh[r, q * 128 : q * 128 + 128] = hi
                rl[r, q * 128 : q * 128 + 128] = lo


def solve_rows(w, n, rh, rl, m, done):
    w00, w10, w11 = split(w[0:256, 0:256]), split(w[256:512, 0:256]), split(w[256:512, 256:512])
    for half in range(2):
        cols = pl.ds(half * 512, 512)
        r0, r1 = (rh[0:256, cols], rl[0:256, cols]), (rh[256:512, cols], rl[256:512, cols])
        t0 = split(mm3(w00, r0))
        t1 = split(mm3(w10, r0) + mm3(w11, r1))
        m[half, 0:256] = mm3(w00, t0, True) + mm3(w10, t1, True)
        m[half, 256:512] = mm3(w11, t1, True)
        for k in range(2):
            @pl.when(n == k)
            def _(k=k):
                m[half, :, 0:128] = -w[pl.ds(k * 256 + half * 128, 128), :].T
        done(half)


def update_tile(out, pan, m, core, t, half, keep):
    o2 = out.reshape(2048 * 8, 128)
    left = [split(pan[k, t, :, core].reshape(512, 256)) for k in range(2)]
    right = [split(m[half, k * 256 : k * 256 + 256]) for k in range(2)]
    prod = mm3(left[0], right[0]) + mm3(left[1], right[1])
    for q in range(4):
        there = pl.ds(t * 512 * 8 + half * 4 + q, 512, stride=8)
        held = o2[there, :]
        if q == 0:
            held = held * keep
        o2[there, :] = held - prod[:, q * 128 : q * 128 + 128]


def own_rows(out, low, row, n):
    o2 = out.reshape(2048 * 8, 128)
    for q in range(8):
        there = pl.ds(q, 256, stride=8)
        if q % 4:
            o2[there, :] = jnp.zeros((256, 128), F32)
        else:
            h = (q // 4) * 128
            @pl.when(row == n)
            def _(there=there, h=h):
                o2[there, :] = low[n, :, h : h + 128]

            @pl.when((row != n) & ((row != 1) | (n != 0)))
            def _(there=there):
                o2[there, :] = jnp.zeros((256, 128), F32)


def kernel(a, out, pan, rows, diag, s, w, low, xa, xi, ta, ti, rh, rl, m, a_sem, *sems):
    net = Net(a, pan, rows, diag, m, low, sems)
    net.start_loads()
    held = pltpu.make_async_copy(a, out, a_sem)
    net.barrier()
    net.own_first()
    source = (net.row == 0) & (net.n == 0)
    pl.when(source)(net.d_source)
    net.own_rest()
    held.start()
    keep = jnp.where(net.n < 2, 0.0, 1.0).astype(F32)

    @pl.when(net.core == 0)
    def _():
        @pl.when(net.x == 0)
        def _():
            net.q_first()
            pl.when(source)(net.d_line)
            pl.when(net.n != 0)(net.d_spread)
            gather_rows(rows, rh, rl)

        pl.when(net.x != 0)(net.q_spread)
        pl.when(net.x != 0)(lambda: net.d_wait(0))
        s[0:256, 0:256] = symmetrise(block(diag, 0))

        def join():
            @pl.when(net.x != 0)
            def _():
                net.q_last()
                gather_rows(rows, rh, rl)
                net.d_wait(1)
                net.d_wait(2)

            return block(diag, 1), block(diag, 2)


        factor512(s, w, xa, xi, ta, ti, join)
        solve_rows(w, net.n, rh, rl, m, lambda i: net.m_copy(i).start())

        @pl.when(net.x == 0)
        def _():
            @pl.when(net.n == 0)
            def _():
                low[0] = transposed_upper(s[0:256, 0:256])

            @pl.when(net.n == 1)
            def _():
                low[1] = transposed_upper(s[256:512, 256:512])
                net.low_copy().start()

    @pl.when(net.core == 1)
    def _():

        def one(i, _):
            net.p_round(i)
            return 0

        lax.fori_loop(0, ROUNDS, one, 0)
    held.wait()

    for half in range(2):
        @pl.when(net.core == 1)
        def _(half=half):
            net.m_copy(half).wait_recv()

        def tile(t, _, half=half):
            if half == 0:
                pl.when(net.core == 0)(lambda: net.p_land(t))
            update_tile(out, pan, m, net.core, t, half, keep)
            return 0

        lax.fori_loop(0, 4, tile, 0)

    held_low = (net.x == 0) & (net.n == 1)

    @pl.when(held_low & (net.core == 1))
    def _():
        net.low_copy().wait_recv()

    @pl.when(net.row < 2)
    def _():
        own_rows(out, low, net.row, net.n)

    @pl.when(net.core == 0)
    def _():
        pl.when(net.x == 0)(net.d_drain)
        net.q_drain()
        for i in range(2):
            net.m_copy(i).wait_send()
        pl.when(held_low)(lambda: net.low_copy().wait_send())

    @pl.when(net.core == 1)
    def _():
        net.p_drain()

    net.own_drain()


def two_steps(a):
    return pl.pallas_call(
        kernel,
        out_shape=pltpu.VMEM(a.shape, F32),
        in_specs=[pl.BlockSpec(memory_space=pl.ANY)],
        out_specs=pl.BlockSpec(memory_space=pltpu.VMEM),
        scratch_shapes=[
            pltpu.VMEM((2, 4, NCH, 2, CH, 256), F32),
            pltpu.VMEM((8, 2, CH, 8, 128), F32),
            pltpu.VMEM((3 * NDU, DU // CH, CH, 256), F32),
            pltpu.VMEM((512, 512), F32),
            pltpu.VMEM((512, 512), F32),
            pltpu.VMEM((2, 256, 256), F32),
        ]
        + [pltpu.VMEM((128, 128), F32)] * 4
        + [pltpu.VMEM((512, 1024), BF16)] * 2
        + [pltpu.VMEM((2, 512, 512), F32), pltpu.SemaphoreType.DMA]
        + list(SEMS),
        compiler_params=pltpu.CompilerParams(
            collective_id=0, has_side_effects=True, vmem_limit_bytes=46 * 2**20
        ),
        name="steps",
    )(a)


def shards(covariance):
    a = covariance.reshape(8, 256, 4, 2, 128).transpose(0, 1, 3, 2, 4).reshape(2048 // CH, CH, 8, 128)
    out = two_steps(a)
    return out.reshape(8, 256, 2, 4, 128).transpose(0, 1, 3, 2, 4).reshape(covariance.shape)


def solution(mesh):
    spec = P("row", None, None, "col", None, None)
    return jax.shard_map(shards, mesh=mesh, in_specs=(spec,), out_specs=spec, check_vma=False)
```

```python
import functools

import jax
import jax.numpy as jnp
from jax import lax
from jax.experimental import pallas as pl
from jax.experimental.pallas import tpu as pltpu
from jax.sharding import PartitionSpec as P

F32 = jnp.float32
BF16 = jnp.bfloat16
HIGHEST = lax.Precision.HIGHEST
MESH = pl.DeviceIdType.MESH

PARENT = (
    (None, 5, 3, 0, 0, 4, 10, 4, 4, 10, 14, 10, 15, 14, 2, 14),
    (None, 2, 3, 0, 5, 9, 7, 3, 12, 8, 11, 7, 0, 9, 10, 11),
    (None, 0, 6, 7, 0, 4, 7, 4, 4, 8, 9, 7, 8, 12, 15, 12),
    (None, 0, 14, 15, 7, 1, 5, 3, 11, 13, 11, 15, 0, 12, 13, 12),
    (1, None, 6, 7, 7, 1, 5, 6, 9, 5, 6, 8, 8, 9, 10, 11),
    (1, None, 1, 15, 5, 6, 2, 6, 11, 5, 14, 15, 15, 14, 2, 14),
    (12, None, 14, 2, 8, 9, 10, 11, 9, 13, 9, 8, 13, 1, 13, 3),
    (3, None, 1, 2, 8, 6, 2, 11, 12, 10, 6, 10, 13, 1, 15, 3),
)
DIRS = ((1, 0), (-1, 0), (0, 1), (0, -1))


def step(n, dy, dz):
    return (n % 4 + dy) % 4 + ((n // 4 + dz) % 4) * 4


def depth_of(tree, n):
    d = 0
    while PARENT[tree][n] is not None:
        n = PARENT[tree][n]
        d += 1
    return d


DEPTH = tuple(tuple(depth_of(t, n) for n in range(16)) for t in range(8))
CHILD = tuple(
    tuple(tuple(int(PARENT[t][step(n, *d)] == n) for n in range(16)) for d in DIRS) for t in range(8)
)
OFFSET = tuple(tuple(5 * d // 2 for d in row) for row in DEPTH)


def pick(n, table):
    value = jnp.int32(table[0])
    for i in range(1, len(table)):
        if table[i] != table[0]:
            value = jnp.where(n == i, jnp.int32(table[i]), value)
    return value


def wrap(v, m):
    return lax.rem(v + m, m)


CH = 32
NCH = 512 // CH
PG = 8
NG = NCH // PG
FIRST = 256 // CH // PG
DU = 64
NDU = 256 // DU
ROUNDS = NCH + max(max(o) for o in OFFSET)


class Net:
    def __init__(self, a, pan, rows, diag, m, low, sems):
        self.a, self.pan, self.rows, self.diag, self.m, self.low = a, pan, rows, diag, m, low
        (self.load, self.seed, self.p_send, self.p_recv, self.g_send, self.g_recv, self.q_send, self.q_recv,
         self.d_send, self.d_recv, self.m_send, self.m_recv) = sems
        self.row = lax.axis_index("row")
        self.n = lax.axis_index("col")
        self.x = self.row // 2
        self.core = lax.rem(self.row, 2)
        self.y = lax.rem(self.n, 4)
        self.z = self.n // 4
        self.other = self.at(dcore=1)
        self.depth = [pick(self.n, DEPTH[t]) for t in range(4)]
        self.offset = [pick(self.n, OFFSET[t]) for t in range(8)]
        self.child = [[pick(self.n, CHILD[t][j]) for j in range(4)] for t in range(8)]

    def at(self, dx=0, dcore=0, dy=0, dz=0):
        return (
            wrap(self.x + dx, 4) * 2 + wrap(self.core + dcore, 2),
            wrap(self.z + dz, 4) * 4 + wrap(self.y + dy, 4),
        )

    def remote(self, part, send, recv, dev, src=None):
        return pltpu.make_async_remote_copy(
            part if src is None else src, part, send, recv, dev, device_id_type=MESH
        )

    def barrier(self):
        sem = pltpu.get_barrier_semaphore()
        peers = [dict(dcore=1)]
        peers += [dict(dx=d) for d in (1, 2, 3)] + [dict(dy=d) for d in (1, 2, 3)] + [dict(dz=d) for d in (1, 2, 3)]
        peers += [dict(dcore=1, dy=1), dict(dcore=1, dy=-1)]
        for p in peers:
            pl.semaphore_signal(sem, inc=1, device_id=self.at(**p), device_id_type=MESH)
        pl.semaphore_wait(sem, len(peers))

    def panel_load(self, k, c, t, g, h):
        return pltpu.make_async_copy(
            self.a.at[pl.ds(t * NCH + g * PG, PG), :, 4 * h, :],
            self.pan.at[k, t, pl.ds(g * PG, PG), c, :, pl.ds(h * 128, 128)],
            self.load.at[t, g, h],
        )

    def row_load(self, k):
        return pltpu.make_async_copy(self.a.at[pl.ds(0, 256 // CH)], self.rows.at[:, k], self.load.at[4, 0, 0])

    def each_own(self, f):
        for k in range(2):
            for c in range(2):
                pl.when((self.n == k) & (self.core == c))(functools.partial(f, k, c))

    def start_loads(self):
        def panel(k, c):
            for g in range(NG):
                for t in range(4):
                    for h in range(2):
                        self.panel_load(k, c, t, g, h).start()

        self.each_own(panel)
        for k in range(2):
            @pl.when(self.row == k)
            def _(k=k):
                self.row_load(k).start()

    def seed_copy(self, k, t, g):
        part = self.pan.at[k, t, pl.ds(g * PG, PG), 0]
        return self.remote(part, self.seed.at[t, g], self.g_recv.at[4 * k + t, g], self.other)

    def d_part(self, u):
        return self.diag.at[u]

    def d_own(self, u):
        per = DU // CH
        return self.pan.at[1 if u // NDU == 2 else 0, 0, pl.ds((u % NDU) * per, per), 0 if u // NDU == 0 else 1]

    def wait_load(self, k, c, t, g):
        for h in range(2):
            self.panel_load(k, c, t, g, h).wait()

    def own_first(self):
        def panel(k, c):
            for g in range(FIRST):
                self.wait_load(k, c, 0, g)
            for d in range(3):
                if (c, k) == ((0, 0), (1, 0), (1, 1))[d]:
                    @pl.when(self.x == 0)
                    def _(d=d):
                        for u in range(d * NDU, d * NDU + NDU):
                            if d == 0:
                                pltpu.make_async_copy(self.d_own(u), self.d_part(u), self.d_recv.at[u]).start()
                            else:
                                self.d_seed(u).start()

        self.each_own(panel)

    def own_rest(self):
        def panel(k, c):
            if c == 0:
                for g in range(NG):
                    for t in range(4):
                        if t > 0 or g >= FIRST:
                            self.wait_load(k, c, t, g)
                        self.seed_copy(k, t, g).start()

        self.each_own(panel)
        @pl.when(self.row == 0)
        def _():
            self.row_load(0).wait()

        @pl.when(self.row == 1)
        def _():
            self.row_load(1).wait()
            self.row_copy().start()

    def row_copy(self):
        part = self.rows.at[:, 1]
        return self.remote(part, self.q_send.at[8], self.q_recv.at[8], self.other)

    def d_seed(self, u):
        return self.remote(self.d_part(u), self.d_send.at[u, 9], self.d_recv.at[u], (0, 0), self.d_own(u))

    def d_copy(self, u, j, dev):
        return self.remote(self.d_part(u), self.d_send.at[u, j], self.d_recv.at[u], dev)

    def d_each(self, t, d, f, tree=True, line=True):
        u = d * NDU + t
        if tree:
            for j, (dy, dz) in enumerate(DIRS):
                @pl.when(self.child[t][j] == 1)
                def _(j=j, dy=dy, dz=dz):
                    f(self.d_copy(u, j, self.at(dy=dy, dz=dz)))
        if line:
            for j, dx in enumerate((1, 3, 2)):
                f(self.d_copy(u, 4 + j, self.at(dx=dx)))

    def d_source(self):
        for d in range(3):
            for t in range(NDU):
                self.d_copy(d * NDU + t, 0, self.other).wait_recv()
                self.d_each(t, d, lambda c: c.start(), line=False)

    def d_line(self):
        for d in range(3):
            for t in range(NDU):
                self.d_each(t, d, lambda c: c.start(), tree=False)

    def d_wait(self, d):
        for t in range(NDU):
            self.d_copy(d * NDU + t, 0, self.other).wait_recv()

    def d_spread(self):
        def one(i, _):
            for t in range(NDU):
                d = i - self.depth[t]

                @pl.when((d >= 0) & (d < 3))
                def _(t=t, d=d):
                    self.d_copy(d * NDU + t, 0, self.other).wait_recv()
                    self.d_each(t, d, lambda c: c.start())

            return 0

        lax.fori_loop(0, 3 + max(max(DEPTH[t]) for t in range(4)), one, 0)

    def d_drain(self):
        def one(d, _):
            for t in range(NDU):
                self.d_each(t, d, lambda c: c.wait_send())
            return 0

        lax.fori_loop(0, 3, one, 0)

    def q_copy(self, u, dev):
        return self.remote(self.rows.at[u], self.q_send.at[u], self.q_recv.at[u], dev)

    def q_on(self, half):
        return (self.x != 3) if half == 0 else (self.x != 1)

    def q_dev(self, half):
        return self.at(dx=1 if half == 0 else -1)

    def q_first(self):
        self.row_copy().wait_recv()
        for c in range(4):
            for half in range(2):
                self.q_copy(half * 4 + c, self.q_dev(half)).start()

    def q_spread(self):
        def one(i, _):
            for half in range(2):
                c = i - (self.x - 1 if half == 0 else 3 - self.x)

                @pl.when((c >= 0) & (c < 4) & self.q_on(half))
                def _(half=half, c=c):
                    u = half * 4 + c
                    self.q_copy(u, self.other).wait_recv()
                    self.q_copy(u, self.q_dev(half)).start()

            return 0

        lax.fori_loop(0, 5, one, 0)

    def q_last(self):
        for half in range(2):
            @pl.when(jnp.logical_not(self.q_on(half)))
            def _(half=half):
                for c in range(4):
                    self.q_copy(half * 4 + c, self.other).wait_recv()

    def q_drain(self):
        for half in range(2):
            @pl.when(self.q_on(half))
            def _(half=half):
                for c in range(4):
                    self.q_copy(half * 4 + c, self.q_dev(half)).wait_send()

    def p_copy(self, t, q, j):
        dy, dz = DIRS[j]
        return self.remote(
            self.pan.at[t // 4, t % 4, q], self.p_send.at[t, j, q], self.p_recv.at[t, q], self.at(dy=dy, dz=dz)
        )

    def p_group(self, t, g):
        part = self.pan.at[t // 4, lax.rem(t, 4), pl.ds(g * PG, PG), 0]
        return self.remote(part, self.g_send.at[t, g], self.g_recv.at[t, g], self.other)

    def is_root(self, t):
        return self.n == t // 4

    def p_ready(self, t, g):
        k = t // 4
        if t % 4 == 0:
            @pl.when(g >= FIRST)
            def _():
                self.wait_load(k, 1, t % 4, g)
        else:
            self.wait_load(k, 1, t % 4, g)
        self.seed_copy(k, t % 4, g).wait_recv()

    def p_round(self, i):
        for t in range(8):
            q = i - self.offset[t]

            @pl.when((q >= 0) & (q < NCH))
            def _(t=t, q=q):
                root = self.is_root(t)

                @pl.when(jnp.logical_not(root))
                def _():
                    self.p_copy(t, q, 0).wait_recv()

                @pl.when(root & (lax.rem(q, PG) == 0))
                def _():
                    self.p_ready(t, q // PG)

                for j in range(4):
                    @pl.when(self.child[t][j] == 1)
                    def _(j=j):
                        self.p_copy(t, q, j).start()

                @pl.when(jnp.logical_not(root) & (lax.rem(q, PG) == PG - 1))
                def _():
                    self.p_group(t, q // PG).start()

    def p_drain(self):
        for t in range(8):
            for j in range(4):
                @pl.when(self.child[t][j] == 1)
                def _(t=t, j=j):
                    def one(q, _):
                        self.p_copy(t, q, j).wait_send()
                        return 0
                    lax.fori_loop(0, NCH, one, 0)

            @pl.when(jnp.logical_not(self.is_root(t)))
            def _(t=t):
                for g in range(NCH // PG):
                    self.p_group(t, g).wait_send()

    def p_land(self, t):
        for k in range(2):
            @pl.when(self.n != k)
            def _(k=k):
                for g in range(NCH // PG):
                    self.p_group(4 * k + t, g).wait_recv()

    def own_drain(self):
        def panel(k, c):
            for d in (1, 2):
                if (c, k) == (1, d - 1):
                    @pl.when(self.x == 0)
                    def _(d=d):
                        for u in range(d * NDU, d * NDU + NDU):
                            self.d_seed(u).wait_send()
            if c == 0:
                for t in range(4):
                    for g in range(NG):
                        self.seed_copy(k, t, g).wait_send()

        self.each_own(panel)

        @pl.when(self.row == 1)
        def _():
            self.row_copy().wait_send()

    def m_copy(self, i):
        return self.remote(self.m.at[i], self.m_send.at[i], self.m_recv.at[i], self.other)

    def low_copy(self):
        return self.remote(self.low.at[1], self.m_send.at[2], self.m_recv.at[2], self.other)


SEMS = (
    pltpu.SemaphoreType.DMA((5, NG, 2)),
    pltpu.SemaphoreType.DMA((4, NG)),
    pltpu.SemaphoreType.DMA((8, 4, NCH)),
    pltpu.SemaphoreType.DMA((8, NCH)),
    pltpu.SemaphoreType.DMA((8, NCH // PG)),
    pltpu.SemaphoreType.DMA((8, NCH // PG)),
    pltpu.SemaphoreType.DMA((9,)),
    pltpu.SemaphoreType.DMA((9,)),
    pltpu.SemaphoreType.DMA((3 * NDU, 10)),
    pltpu.SemaphoreType.DMA((3 * NDU,)),
    pltpu.SemaphoreType.DMA((3,)),
    pltpu.SemaphoreType.DMA((3,)),
)


def split(x):
    hi = x.astype(BF16)
    return hi, (x - hi.astype(F32)).astype(BF16)


def mm(a, b, ta=False, precision=None):
    return lax.dot_general(
        a, b, (((0 if ta else 1,), (0,)), ((), ())), preferred_element_type=F32, precision=precision
    )


def mm3(a, b, ta=False):
    (ah, al), (bh, bl) = a, b
    return mm(ah, bh, ta) + (mm(ah, bl, ta) + mm(al, bh, ta))


def factor128(xa, xi, ta, ti):
    sub = lax.broadcasted_iota(jnp.int32, (8, 128), 0)

    def row(v, p):
        return jnp.broadcast_to(v[p : p + 1, :], (8, 128))

    def lane(v, c):
        return jnp.broadcast_to(v[:, c : c + 1], (8, 128))

    def total(s):
        return ((s[0] + s[1]) + (s[2] + s[3])) + ((s[4] + s[5]) + (s[6] + s[7]))

    first = xa[0:8, :]
    col = [lane(first, k) for k in range(8)]
    for j in range(16):
        here = pl.ds(8 * j, 8)
        ra, ri = xa[here, :], xi[here, :]
        last = j == 15
        if not last:
            nxt = xa[pl.ds(8 * j + 8, 8), :]
            b = [lane(nxt, 8 * j + k) for k in range(8)]
            ahead = [lane(nxt, 8 * j + 8 + k) for k in range(8)]
            below = list(b)
        la = jnp.zeros((8, 128), F32)
        li, rd = la, la
        for p in range(8):
            d = row(col[p], p)
            inv, root = 1.0 / d, lax.rsqrt(d)
            m = jnp.where(sub == p, 0.0, col[p] * inv)
            pa, pi = row(ra, p), row(ri, p)
            if p < 7:
                head = [row(col[k], p) for k in range(p + 1, 8)]
                for k in range(p + 1, 8):
                    col[k] = col[k] - m * head[k - p - 1]
            if not last:
                mb = b[p] * inv
                for k in range(p + 1, 8):
                    b[k] = b[k] - mb * head[k - p - 1]
                for k in range(8):
                    ahead[k] = ahead[k] - mb * row(b[p], k)
            la = jnp.where(sub == p, pa * root, la)
            li = jnp.where(sub == p, pi * root, li)
            rd = jnp.where(sub == p, inv, rd)
            ra, ri = ra - m * pa, ri - m * pi
        ta[here, :], ti[here, :] = la, li
        if not last:
            va, vi = ra * rd, ri * rd
            va = [row(va, k) for k in range(8)]
            vi = [row(vi, k) for k in range(8)]
            for g in range(j + 1, 16):
                there = pl.ds(8 * g, 8)
                xg = xa[there, :]
                c = below if g == j + 1 else [lane(xg, 8 * j + k) for k in range(8)]
                xa[there, :] = xg - total([c[k] * va[k] for k in range(8)])
                xi[there, :] = xi[there, :] - total([c[k] * vi[k] for k in range(8)])
            col = ahead


def factor512(s, w, xa, xi, ta, ti, join):
    w[...] = jnp.zeros((512, 512), F32)
    i0 = lax.broadcasted_iota(jnp.int32, (128, 128), 0)
    i1 = lax.broadcasted_iota(jnp.int32, (128, 128), 1)

    def body(b, _):
        here = pl.ds(pl.multiple_of(b * 128, 128), 128)
        xa[...] = s[here, here]
        xi[...] = jnp.where(i0 == i1, 1.0, 0.0).astype(F32)
        factor128(xa, xi, ta, ti)
        w[here, here] = ti[...]
        s[here, here] = jnp.where(i1 >= i0, ta[...], 0.0)
        for bb in range(4):
            @pl.when(b == bb)
            def _(bb=bb):
                n0, n1 = bb * 128, bb * 128 + 128
                r, rest = pl.ds(n0, 128), pl.ds(n1, 128)
                inv = ti[...]
                if bb > 0:
                    w[r, 0:n0] = mm(inv, w[r, 0:n0], precision=HIGHEST)
                if bb % 2 == 0:
                    u = mm(inv, s[r, rest], precision=HIGHEST)
                    s[r, rest] = u
                    s[rest, rest] = s[rest, rest] - mm(u, u, True, HIGHEST)
                    w[rest, 0:n1] = w[rest, 0:n1] - mm(u, w[r, 0:n1], True, HIGHEST)
                if bb == 1:
                    below, corner = join()
                    first = w[0:256, 0:256]
                    u = mm(first, below.T, precision=HIGHEST)
                    s[256:512, 256:512] = symmetrise(corner) - mm(u, u, True, HIGHEST)
                    w[256:512, 0:256] = -mm(u, first, True, HIGHEST)
        return 0

    lax.fori_loop(0, 4, body, 0)


def transposed_upper(s):
    i0 = lax.broadcasted_iota(jnp.int32, (256, 256), 0)
    i1 = lax.broadcasted_iota(jnp.int32, (256, 256), 1)
    return jnp.where(i1 >= i0, s, 0.0).T


def symmetrise(x):
    return (x + x.T) * 0.5


def block(diag, d):
    return diag[d * NDU : d * NDU + NDU].reshape(256, 256)


def gather_rows(rows, rh, rl):
    flat = rows.reshape(8 * 2 * CH * 8, 128)
    for k in range(2):
        for u in range(8):
            r = pl.ds(k * 256 + u * CH, CH)
            for q in range(8):
                hi, lo = split(flat[pl.ds((u * 2 + k) * CH * 8 + q, CH, stride=8), :])
                rh[r, q * 128 : q * 128 + 128] = hi
                rl[r, q * 128 : q * 128 + 128] = lo


def solve_rows(w, n, rh, rl, m, done):
    w00, w10, w11 = split(w[0:256, 0:256]), split(w[256:512, 0:256]), split(w[256:512, 256:512])
    for half in range(2):
        cols = pl.ds(half * 512, 512)
        r0, r1 = (rh[0:256, cols], rl[0:256, cols]), (rh[256:512, cols], rl[256:512, cols])
        t0 = split(mm3(w00, r0))
        t1 = split(mm3(w10, r0) + mm3(w11, r1))
        m[half, 0:256] = mm3(w00, t0, True) + mm3(w10, t1, True)
        m[half, 256:512] = mm3(w11, t1, True)
        for k in range(2):
            @pl.when(n == k)
            def _(k=k):
                m[half, :, 0:128] = -w[pl.ds(k * 256 + half * 128, 128), :].T
        done(half)


def update_tile(out, pan, m, core, t, half, keep):
    o2 = out.reshape(2048 * 8, 128)
    left = [split(pan[k, t, :, core].reshape(512, 256)) for k in range(2)]
    right = [split(m[half, k * 256 : k * 256 + 256]) for k in range(2)]
    prod = mm3(left[0], right[0]) + mm3(left[1], right[1])
    for q in range(4):
        there = pl.ds(t * 512 * 8 + half * 4 + q, 512, stride=8)
        held = o2[there, :]
        if q == 0:
            held = held * keep
        o2[there, :] = held - prod[:, q * 128 : q * 128 + 128]


def own_rows(out, low, row, n):
    o2 = out.reshape(2048 * 8, 128)
    for q in range(8):
        there = pl.ds(q, 256, stride=8)
        if q % 4:
            o2[there, :] = jnp.zeros((256, 128), F32)
        else:
            h = (q // 4) * 128
            @pl.when(row == n)
            def _(there=there, h=h):
                o2[there, :] = low[n, :, h : h + 128]

            @pl.when((row != n) & ((row != 1) | (n != 0)))
            def _(there=there):
                o2[there, :] = jnp.zeros((256, 128), F32)


def kernel(a, out, pan, rows, diag, s, w, low, xa, xi, ta, ti, rh, rl, m, a_sem, *sems):
    net = Net(a, pan, rows, diag, m, low, sems)
    net.start_loads()
    held = pltpu.make_async_copy(a, out, a_sem)
    net.barrier()
    net.own_first()
    source = (net.row == 0) & (net.n == 0)
    pl.when(source)(net.d_source)
    net.own_rest()
    held.start()
    keep = jnp.where(net.n < 2, 0.0, 1.0).astype(F32)

    @pl.when(net.core == 0)
    def _():
        @pl.when(net.x == 0)
        def _():
            net.q_first()
            pl.when(source)(net.d_line)
            pl.when(net.n != 0)(net.d_spread)
            gather_rows(rows, rh, rl)

        pl.when(net.x != 0)(net.q_spread)
        pl.when(net.x == 2)(lambda: gather_rows(rows, rh, rl))
        pl.when(net.x != 0)(lambda: net.d_wait(0))
        s[0:256, 0:256] = symmetrise(block(diag, 0))

        def join():
            @pl.when(net.x != 0)
            def _():
                net.q_last()
                pl.when(net.x != 2)(lambda: gather_rows(rows, rh, rl))
                net.d_wait(1)
                net.d_wait(2)

            return block(diag, 1), block(diag, 2)


        factor512(s, w, xa, xi, ta, ti, join)
        solve_rows(w, net.n, rh, rl, m, lambda i: net.m_copy(i).start())

        @pl.when(net.x == 0)
        def _():
            @pl.when(net.n == 0)
            def _():
                low[0] = transposed_upper(s[0:256, 0:256])

            @pl.when(net.n == 1)
            def _():
                low[1] = transposed_upper(s[256:512, 256:512])
                net.low_copy().start()

    @pl.when(net.core == 1)
    def _():

        def one(i, _):
            net.p_round(i)
            return 0

        lax.fori_loop(0, ROUNDS, one, 0)
    held.wait()

    for half in range(2):
        @pl.when(net.core == 1)
        def _(half=half):
            net.m_copy(half).wait_recv()

        def tile(t, _, half=half):
            if half == 0:
                pl.when(net.core == 0)(lambda: net.p_land(t))
            update_tile(out, pan, m, net.core, t, half, keep)
            return 0

        lax.fori_loop(0, 4, tile, 0)

    held_low = (net.x == 0) & (net.n == 1)

    @pl.when(held_low & (net.core == 1))
    def _():
        net.low_copy().wait_recv()

    @pl.when(net.row < 2)
    def _():
        own_rows(out, low, net.row, net.n)

    @pl.when(net.core == 0)
    def _():
        pl.when(net.x == 0)(net.d_drain)
        net.q_drain()
        for i in range(2):
            net.m_copy(i).wait_send()
        pl.when(held_low)(lambda: net.low_copy().wait_send())

    @pl.when(net.core == 1)
    def _():
        net.p_drain()

    net.own_drain()


def two_steps(a):
    return pl.pallas_call(
        kernel,
        out_shape=pltpu.VMEM(a.shape, F32),
        in_specs=[pl.BlockSpec(memory_space=pl.ANY)],
        out_specs=pl.BlockSpec(memory_space=pltpu.VMEM),
        scratch_shapes=[
            pltpu.VMEM((2, 4, NCH, 2, CH, 256), F32),
            pltpu.VMEM((8, 2, CH, 8, 128), F32),
            pltpu.VMEM((3 * NDU, DU // CH, CH, 256), F32),
            pltpu.VMEM((512, 512), F32),
            pltpu.VMEM((512, 512), F32),
            pltpu.VMEM((2, 256, 256), F32),
        ]
        + [pltpu.VMEM((128, 128), F32)] * 4
        + [pltpu.VMEM((512, 1024), BF16)] * 2
        + [pltpu.VMEM((2, 512, 512), F32), pltpu.SemaphoreType.DMA]
        + list(SEMS),
        compiler_params=pltpu.CompilerParams(
            collective_id=0, has_side_effects=True, vmem_limit_bytes=46 * 2**20
        ),
        name="steps",
    )(a)


def shards(covariance):
    a = covariance.reshape(8, 256, 4, 2, 128).transpose(0, 1, 3, 2, 4).reshape(2048 // CH, CH, 8, 128)
    out = two_steps(a)
    return out.reshape(8, 256, 2, 4, 128).transpose(0, 1, 3, 2, 4).reshape(covariance.shape)


def solution(mesh):
    spec = P("row", None, None, "col", None, None)
    return jax.shard_map(shards, mesh=mesh, in_specs=(spec,), out_specs=spec, check_vma=False)
```
